32 devices in a mesh: groups: 2 (over x), docs: 16 (over z, y, core).
Axes of the slice: x: 2, y: 2, z: 4, core: 2. Of those that a mesh axis runs over, the one named last changes fastest.
Arguments:
- prompt_queries: bfloat16 [4096, 8192], P(('groups', 'docs')), parts along dimension 0, may hold values from -24 to 24
- prompt_keys: bfloat16 [4096, 512], P(('groups', 'docs')), parts along dimension 0, may hold values from -6 to 6
- prompt_values: bfloat16 [4096, 512], P(('groups', 'docs')), parts along dimension 0, may hold values from -6 to 6
- cache_keys: bfloat16 [16384, 512], P(('groups', 'docs')), parts along dimension 0, may hold values from -24 to 24
- cache_values: bfloat16 [16384, 512], P(('groups', 'docs')), parts along dimension 0, may hold values from -6 to 6
- doc_blocks: int32 [16], P('groups'), parts along dimension 0, may hold values from 1 to 63, as said below
- reader_docs: int32 [32], P(('groups', 'docs')), parts along dimension 0, may hold values from 0 to 7, as said below
- reader_offsets: int32 [32], P(('groups', 'docs')), parts along dimension 0, may hold values from 0 to 4095
Outputs:
- attended: bfloat16 [4096, 8192], P(('groups', 'docs')), parts along dimension 0
The draws below stay inside these ranges and needn't reach their ends.
There are 2 independent parts, one for each index of `groups`. The reference program is written for one: setup_inputs(seed, part) draws one part's arguments, and reference() takes and returns one part's arrays. A program takes and returns all parts, laid end to end along the dimension named above; each array names one. Nothing has to cross between parts.
Inputs may be any that keep to these rules, and one draw needn't show every extreme that they name: `doc_blocks`: the lengths sum to 256; the longest is exactly 63. `reader_docs`: reader r's document holds one or more of the blocks r * 16 to (r + 1) * 16 - 1.
All inputs are finite; a program needn't handle non-finite values.
Results may differ from the reference program's by a relative error of at most 0.012.
The reference program's roundings to bfloat16 on the way count: a program that leaves them out, or rounds other values in their place, can miss the bound.
Values may be sent and summed in bfloat16 or wider, within the bound.
No kernel may reach another device: no remote copies, remote signals or barrier semaphores. Data moves between devices by JAX's collectives and lax.ppermute only.
A program may use at most 128 MiB of HBM per device.

```python
import math
import jax
import jax.numpy as jnp
from jax import lax

QH = 64
KVH = 4
HD = 128
ROWS = 128
BLK = 32
BLK_DEV = 16
READERS = 16
CACHE = 8192
NDOC = 8
MAXDOC = 63


def document_layout(key):
    pairs = NDOC // 2
    quad = 4 * BLK_DEV
    lead = jax.random.randint(jax.random.fold_in(key, 11), (pairs,), 1, quad)
    chosen = jax.random.randint(jax.random.fold_in(key, 12), (), 0, pairs)
    lead = jnp.where(jnp.arange(pairs) == chosen, quad - 1, lead)
    lengths = jnp.stack([lead, quad - lead], axis=1).reshape(NDOC)
    return jax.random.permutation(jax.random.fold_in(key, 13), lengths).astype(jnp.int32)


def draw_doc_blocks(key, part):
    return document_layout(key)


def draw_reader_docs(key, part):
    lengths = document_layout(key)
    ends = jnp.cumsum(lengths).astype(jnp.int32)
    reader = jnp.arange(READERS, dtype=jnp.int32)
    picks = reader * BLK_DEV + jax.random.randint(jax.random.fold_in(key, 21), (READERS,), 0, BLK_DEV)
    return jnp.sum((ends[None, :] <= picks[:, None]).astype(jnp.int32), axis=1).astype(jnp.int32)


def draw_cache_keys(key, part):
    base = jax.random.normal(key, (CACHE, KVH * HD), jnp.float32)
    return jnp.clip(base, -24.0, 24.0).astype(jnp.bfloat16)


def draw_prompt_queries(key, part):
    base = jax.random.normal(key, (READERS * ROWS, QH * HD), jnp.float32)
    return jnp.clip(base, -24.0, 24.0).astype(jnp.bfloat16)


def set_ends(values, rng, low, top_value):
    extent = values.shape
    spot = [jax.random.randint(jax.random.fold_in(rng, axis), (), 0, extent[axis]) for axis in range(len(extent))]
    values = values.at[tuple(spot)].set(low)
    longest = extent.index(max(extent))
    spot[longest] = (spot[longest] + 1) % extent[longest]
    return values.at[tuple(spot)].set(top_value)


def block_scale(own_key, shape, shards, low, largest):
    gain = 1.0
    for position, blocks in shards:
        steps = jax.random.uniform(jax.random.fold_in(jax.random.fold_in(own_key, 6), position), (blocks,), jnp.float32, low / len(shards), largest / len(shards))
        gain = gain * jnp.repeat(jnp.exp(steps), shape[position] // blocks).reshape((-1,) + (1,) * (len(shape) - 1 - position))
    return gain


def noise(rng, shape, scale, most, split=(), kind=jnp.bfloat16):
    values = jax.random.normal(rng, shape, jnp.float32) * scale
    if len(split) > 0:
        values = block_scale(rng, shape, split, -0.22, 0.18) * values
    return jnp.clip(values, min=-most, max=most).astype(kind)


def setup_inputs(seed: int = 0, part: int = 0) -> dict:
    seeds = jax.random.split(jax.random.key(seed), 9)
    part_splits = jax.random.split(jax.random.fold_in(seeds[8], part), 9)
    prompt_queries = draw_prompt_queries(jax.random.fold_in(jax.random.fold_in(seeds[8], part), 71), part)
    prompt_keys = noise(part_splits[1], (READERS * ROWS, KVH * HD), 1.0, 6.0, ((0, 16),))
    prompt_values = noise(part_splits[2], (READERS * ROWS, KVH * HD), 1.0, 6.0, ((0, 16),))
    cache_keys = draw_cache_keys(jax.random.fold_in(jax.random.fold_in(seeds[8], part), 71), part)
    cache_values = noise(part_splits[4], (CACHE, KVH * HD), 1.0, 6.0, ((0, 16),))
    doc_blocks = draw_doc_blocks(jax.random.fold_in(jax.random.fold_in(seeds[8], part), 71), part)
    reader_docs = draw_reader_docs(jax.random.fold_in(jax.random.fold_in(seeds[8], part), 71), part)
    reader_offsets = set_ends(jax.random.randint(part_splits[7], (READERS,), 0, 4096), jax.random.fold_in(part_splits[7], 1), 0, 4095).astype(jnp.int32)
    return dict(prompt_queries=prompt_queries, prompt_keys=prompt_keys, prompt_values=prompt_values, cache_keys=cache_keys, cache_values=cache_values, doc_blocks=doc_blocks, reader_docs=reader_docs, reader_offsets=reader_offsets)


rope_base = 1000000.0
yarn_factor = 4.0
pretrain_context = 32768.0
beta_fast = 32.0
beta_slow = 1.0
attention_gain = 0.1 * math.log(4.0) + 1.0
masked_score = -1e+30

def yarn_table(head_size):
    half_size = head_size // 2

    def correction(turns):
        return head_size * math.log(pretrain_context / (turns * 2.0 * math.pi)) / (2.0 * math.log(rope_base))
    lower = max(math.floor(correction(beta_fast)), 0)
    upper = min(math.ceil(correction(beta_slow)), head_size - 1)
    span_width = max(upper - lower, 0.001)
    table = []
    for column in range(half_size):
        base_freq = rope_base ** (-2.0 * column / head_size)
        fraction = min(max((column - lower) / span_width, 0.0), 1.0)
        table.append(base_freq * fraction / yarn_factor + base_freq * (1.0 - fraction))
    return table

def rotate(vectors, positions):
    head_size = vectors.shape[-1]
    half_size = head_size // 2
    inverse = jnp.asarray(yarn_table(head_size), jnp.float32)
    angles = positions.astype(jnp.float32)[:, None] * inverse[None, :]
    cosine = (jnp.cos(angles) * attention_gain)[:, None, :]
    sine = (jnp.sin(angles) * attention_gain)[:, None, :]
    first_half = vectors[..., :half_size]
    second_half = vectors[..., half_size:]
    return jnp.concatenate([first_half * cosine - second_half * sine, second_half * cosine + first_half * sine], axis=-1)

def settle(values):
    return lax.optimization_barrier(values.astype(jnp.bfloat16)).astype(jnp.float32)

def reference(prompt_queries, prompt_keys, prompt_values, cache_keys, cache_values, doc_blocks, reader_docs, reader_offsets):
    repeat = QH // KVH
    window_rows = MAXDOC * BLK
    score_scale = 1.0 / math.sqrt(HD)
    ends = jnp.cumsum(doc_blocks).astype(jnp.int32)
    starts = (ends - doc_blocks).astype(jnp.int32)
    filler = jnp.zeros((window_rows, KVH * HD), cache_keys.dtype)
    long_keys = jnp.concatenate([cache_keys, filler], axis=0)
    long_values = jnp.concatenate([cache_values, filler], axis=0)
    row_index = jnp.arange(ROWS, dtype=jnp.int32)
    positions = jnp.arange(window_rows, dtype=jnp.int32)

    def one_reader(reader):
        first_row = (reader * ROWS).astype(jnp.int32)
        queries = lax.dynamic_slice_in_dim(prompt_queries, first_row, ROWS, 0).astype(jnp.float32).reshape(ROWS, QH, HD)
        own_keys = lax.dynamic_slice_in_dim(prompt_keys, first_row, ROWS, 0).astype(jnp.float32).reshape(ROWS, KVH, HD)
        own_values = lax.dynamic_slice_in_dim(prompt_values, first_row, ROWS, 0).astype(jnp.float32).reshape(ROWS, KVH, HD)
        document = reader_docs[reader]
        start_position = reader_offsets[reader]
        first_token = (starts[document] * BLK).astype(jnp.int32)
        length = doc_blocks[document] * BLK
        doc_keys = lax.dynamic_slice_in_dim(long_keys, first_token, window_rows, 0).astype(jnp.float32).reshape(window_rows, KVH, HD)
        doc_values = lax.dynamic_slice_in_dim(long_values, first_token, window_rows, 0).astype(jnp.float32).reshape(window_rows, KVH, HD)
        turned = settle(rotate(queries, start_position + row_index)).reshape(ROWS, KVH, repeat, HD)
        self_keys = settle(rotate(own_keys, start_position + row_index))
        far_keys = settle(rotate(doc_keys, positions))
        near_scores = jnp.einsum('gkrd,tkd->gkrt', turned, self_keys) * score_scale
        far_scores = jnp.einsum('gkrd,tkd->gkrt', turned, far_keys) * score_scale
        near_visible = (row_index[None, :] <= row_index[:, None])[:, None, None, :]
        far_visible = (positions < length)[None, None, None, :]
        near_scores = jnp.where(near_visible, near_scores, masked_score)
        far_scores = jnp.where(far_visible, far_scores, masked_score)
        peak = jnp.maximum(lax.optimization_barrier(jnp.max(near_scores, axis=-1)), lax.optimization_barrier(jnp.max(far_scores, axis=-1)))
        near_weights = jnp.where(near_visible, jnp.exp(near_scores - peak[..., None]), 0.0)
        far_weights = jnp.where(far_visible, jnp.exp(far_scores - peak[..., None]), 0.0)
        denominator = lax.optimization_barrier(jnp.sum(near_weights, axis=-1)) + lax.optimization_barrier(jnp.sum(far_weights, axis=-1))
        weighted = jnp.einsum('gkrt,tkd->gkrd', settle(near_weights), own_values) + jnp.einsum('gkrt,tkd->gkrd', settle(far_weights), doc_values)
        return (weighted / denominator[..., None]).astype(jnp.bfloat16).reshape(ROWS, QH * HD)
    results = lax.map(one_reader, jnp.arange(READERS, dtype=jnp.int32))
    return results.reshape(READERS * ROWS, QH * HD)
```

```python
import functools
import math

import jax
import jax.numpy as jnp
import numpy as np
from jax import lax
from jax.experimental import pallas as pl
from jax.experimental.pallas import tpu as pltpu
from jax.sharding import PartitionSpec as P

HD = 128
BLK = 32
HALF_KV = 2
F32 = jnp.float32
BF16 = jnp.bfloat16

rope_base = 1000000.0
yarn_factor = 4.0
pretrain_context = 32768.0
beta_fast = 32.0
beta_slow = 1.0
attention_gain = 0.1 * math.log(4.0) + 1.0
score_scale = 1.0 / math.sqrt(HD)
EXP2_SCALE = score_scale * math.log2(math.e)
SAFE_LOG2 = 64.0
masked_score = -1e30
ROW_TILE_HEADS = 4
VMEM = 56 * 1024 * 1024


def yarn_table():
    half = HD // 2

    def correction(turns):
        return (
            HD * math.log(pretrain_context / (turns * 2.0 * math.pi)) / (2.0 * math.log(rope_base))
        )

    lower = max(math.floor(correction(beta_fast)), 0)
    upper = min(math.ceil(correction(beta_slow)), HD - 1)
    span_width = max(upper - lower, 0.001)
    table = []
    for column in range(half):
        base_freq = rope_base ** (-2.0 * column / HD)
        fraction = min(max((column - lower) / span_width, 0.0), 1.0)
        table.append(base_freq * fraction / yarn_factor + base_freq * (1.0 - fraction))
    return np.asarray(table, np.float32).astype(np.float64)


def angle_rows(positions, gain):
    angles = np.asarray(positions, np.float64)[:, None] * yarn_table()[None, :]
    cosine = np.cos(angles) * gain
    sine = np.sin(angles) * gain
    return (
        np.concatenate([cosine, cosine], axis=1).astype(np.float32),
        np.concatenate([-sine, sine], axis=1).astype(np.float32),
    )


COARSE = 64


def turn(x, c1, s1, c2, s2):
    cosine = c1 * c2 - s1 * s2
    sine = s1 * c2 + c1 * s2
    return x * cosine + pltpu.roll(x, HD // 2, 1) * sine


def cache_kernel(ids, doc_blocks, bc, bs, tc, ts, k_ref, v_ref, mine_ref, theirs_ref):
    half = ids[0]
    first_block = ids[1]
    ndoc = doc_blocks.shape[0]
    width = HALF_KV * HD
    step = pl.program_id(0)
    blocks = k_ref.shape[0] // BLK
    c2 = tc[0:BLK, :]
    s2 = ts[0:BLK, :]
    for b in range(blocks):
        block = first_block + step * blocks + b

        def find(d, carry):
            start, begin = carry
            end = start + doc_blocks[d]
            return (end, jnp.where(start <= block, start, begin))

        _, begin = lax.fori_loop(0, ndoc, find, (jnp.int32(0), jnp.int32(0)), unroll=True)
        place = jnp.clip(block - begin, 0, COARSE - 1)
        c1 = bc[pl.ds(place, 1), :]
        s1 = bs[pl.ds(place, 1), :]
        cosine = c1 * c2 - s1 * s2
        sine = s1 * c2 + c1 * s2
        rows = pl.ds(b * BLK, BLK)
        for out, which in ((mine_ref, half), (theirs_ref, 1 - half)):
            for j in range(HALF_KV):
                col = pl.multiple_of(which * width + j * HD, HD)
                x = k_ref[rows, pl.ds(col, HD)].astype(F32)
                y = x * cosine + pltpu.roll(x, HD // 2, 1) * sine
                out[rows, pl.ds(j * HD, HD)] = y.astype(BF16)
    for out, which in ((mine_ref, half), (theirs_ref, 1 - half)):
        col = pl.multiple_of(which * width, HD)
        out[:, pl.ds(width, width)] = v_ref[:, pl.ds(col, width)]


def prepare_cache(ids, doc_blocks, tables, keys, values):
    tokens, columns = keys.shape
    steps = 4
    whole = lambda shape: pl.BlockSpec(shape, lambda i, *_: (0, 0))
    part = pl.BlockSpec((tokens // steps, columns), lambda i, *_: (i, 0))
    out = pl.BlockSpec((tokens // steps, columns), lambda i, *_: (i, 0))
    return pl.pallas_call(
        cache_kernel,
        grid_spec=pltpu.PrefetchScalarGridSpec(
            num_scalar_prefetch=2,
            grid=(steps,),
            in_specs=[whole(t.shape) for t in tables] + [part, part],
            out_specs=[out, out],
        ),
        out_shape=[jax.ShapeDtypeStruct((tokens, columns), BF16)] * 2,
        cost_estimate=pl.CostEstimate(flops=4000000, bytes_accessed=4 << 20, transcendentals=0),
        name="prepare_cache",
    )(ids, doc_blocks, *tables, keys, values)


def query_kernel(sel, offset, doc, ac, asn, tc, ts, q_ref, k_ref, v_ref, out_ref):
    step = pl.program_id(0)
    rows, columns = q_ref.shape
    off = jnp.clip(offset[0], 0, COARSE * COARSE - 1)
    hi = off // COARSE
    lo = off - hi * COARSE
    ca, sa = ac[pl.ds(hi, 1), :], asn[pl.ds(hi, 1), :]
    cb, sb = tc[pl.ds(lo, 1), :], ts[pl.ds(lo, 1), :]
    c1 = ca * cb - sa * sb
    s1 = sa * cb + ca * sb
    c2, s2 = tc[0:rows, :], ts[0:rows, :]
    cosine = c1 * c2 - s1 * s2
    sine = s1 * c2 + c1 * s2

    def rotated(x):
        x = x.astype(F32)
        return (x * cosine + pltpu.roll(x, HD // 2, 1) * sine).astype(BF16)

    for h in range(columns // HD):
        col = pl.multiple_of(step * columns + h * HD, HD)
        out_ref[:, pl.ds(col, HD)] = rotated(q_ref[:, h * HD : (h + 1) * HD])

    @pl.when(step == 0)
    def _():
        base = out_ref.shape[1] - (2 * HALF_KV + 1) * HD
        for j in range(HALF_KV):
            out_ref[:, base + j * HD : base + (j + 1) * HD] = rotated(
                k_ref[:, j * HD : (j + 1) * HD]
            )
        base += HALF_KV * HD
        out_ref[:, base : base + HALF_KV * HD] = v_ref[...]
        base += HALF_KV * HD
        out_ref[:, base : base + HD] = jnp.full((rows, HD), doc[0].astype(F32), F32).astype(BF16)


def prepare_queries(which, offset, doc, tables, queries, keys, values):
    rows, columns = queries.shape
    mine = columns // 2
    steps = 4
    block = mine // steps
    width = HALF_KV * HD
    whole = lambda shape: pl.BlockSpec(shape, lambda i, *_: (0, 0))
    kv = pl.BlockSpec((rows, width), lambda i, sel, *_: (0, sel[0]))
    total = mine + 2 * width + HD
    return pl.pallas_call(
        query_kernel,
        grid_spec=pltpu.PrefetchScalarGridSpec(
            num_scalar_prefetch=3,
            grid=(steps,),
            in_specs=[whole(t.shape) for t in tables]
            + [pl.BlockSpec((rows, block), lambda i, sel, *_: (0, sel[0] * steps + i)), kv, kv],
            out_specs=pl.BlockSpec((rows, total), lambda i, *_: (0, 0)),
        ),
        out_shape=jax.ShapeDtypeStruct((rows, total), BF16),
        cost_estimate=pl.CostEstimate(flops=6000000, bytes_accessed=3 << 20, transcendentals=0),
        name="prepare_queries",
    )(which, offset, doc, *tables, queries, keys, values)


def scores_of(q, k):
    return lax.dot_general(q, k, (((1,), (1,)), ((), ())), preferred_element_type=F32)


def square_bound(x):
    x = x.astype(F32)
    return jnp.max(jnp.sum(x * x, axis=1, keepdims=True))


def span_of(doc_blocks, doc):
    def find(d, carry):
        total, start, end = carry
        size = doc_blocks[d]
        start = jnp.where(d == doc, total, start)
        end = jnp.where(d == doc, total + size, end)
        return (total + size, start, end)

    zero = jnp.int32(0)
    _, start, end = lax.fori_loop(0, doc_blocks.shape[0], find, (zero, zero, zero), unroll=True)
    return start * BLK, end * BLK


def causal_mask(n):
    return lax.broadcasted_iota(jnp.int32, (n, n), 1) <= lax.broadcasted_iota(jnp.int32, (n, n), 0)


def stage_kernel(nr, npieces, first, last, nall, *refs):
    refs = list(refs)
    take = lambda n: [refs.pop(0) for _ in range(n)]
    doc_blocks, bases = take(2)
    if last:
        (all_bases,) = take(1)
    readers = [take(4) for _ in range(nr)]
    pieces = [take(2) for _ in range(npieces)]
    if not first:
        acc_in, bound_in = take(2)
    if last:
        everything = take(nall)
        outs = take(nr)
        acc_ref = refs.pop(0)
        kbuf, vbuf, peak_ref, total_ref, sem = take(5)
    else:
        acc_ref, bound_ref = take(2)
    kvh = pl.program_id(0)
    rows = readers[0][0].shape[0]
    heads = readers[0][0].shape[1] // HD
    tile = ROW_TILE_HEADS * rows
    tiles = heads // ROW_TILE_HEADS
    ones = jnp.ones((rows, HD), BF16)

    for r, (q_ref, k_ref, v_ref, d_ref) in enumerate(readers):
        document = jnp.max(d_ref[0:16, :].astype(F32)).astype(jnp.int32)
        start, end = span_of(doc_blocks, document)
        acc = acc_ref.at[r, 0]

        def q_tile(t, q_ref=q_ref):
            return jnp.concatenate(
                [
                    q_ref[:, pl.ds(pl.multiple_of((t * ROW_TILE_HEADS + g) * HD, HD), HD)]
                    for g in range(ROW_TILE_HEADS)
                ],
                axis=0,
            )

        if first:
            own_k = k_ref[...]
            own_v = jnp.concatenate([v_ref[...], ones], axis=1)
            mask = causal_mask(rows)
            mask = jnp.concatenate([mask] * ROW_TILE_HEADS, axis=0)
            bound = square_bound(own_k)

            def self_tile(t, q_most, own_k=own_k, own_v=own_v, mask=mask, acc=acc):
                q = q_tile(t)
                weights = jnp.exp2(scores_of(q, own_k) * EXP2_SCALE)
                weights = jnp.where(mask, weights, 0.0).astype(BF16)
                acc[pl.ds(pl.multiple_of(t * tile, tile), tile), :] = jnp.dot(
                    weights, own_v, preferred_element_type=F32
                )
                return jnp.maximum(q_most, square_bound(q))

            q_most = lax.fori_loop(0, tiles, self_tile, jnp.float32(0.0))
            bound_ref[r, 0, 0:8, :] = jnp.full((8, HD), bound, F32)
            bound_ref[r, 0, 8:16, :] = jnp.full((8, HD), q_most, F32)
            bounds = bound_ref
        elif last:
            acc[...] = acc_in[r, 0]
        else:
            acc[...] = acc_in[r, 0]
            bound_ref[...] = bound_in[...]

        extra = [jnp.float32(0.0)]
        for p, (kp, vp) in enumerate(pieces):
            base = bases[p]
            count = kp.shape[0]
            seen = (base < end) & (base + count > start)

            @pl.when(seen)
            def _(kp=kp, vp=vp, base=base, count=count, r=r, acc=acc, start=start, end=end):
                token = base + lax.broadcasted_iota(jnp.int32, (count, HD), 0)
                shown = (token >= start) & (token < end)
                keys = kp[...]
                values = jnp.where(shown, vp[...].astype(F32), 0.0).astype(BF16)
                values = jnp.concatenate([values, shown.astype(F32).astype(BF16)], axis=1)
                if not last:
                    bound_ref[r, 0, 0:8, :] = jnp.maximum(
                        bound_ref[r, 0, 0:8, :], square_bound(keys)
                    )

                def body(t, _):
                    weights = jnp.exp2(scores_of(q_tile(t), keys) * EXP2_SCALE).astype(BF16)
                    at = pl.ds(pl.multiple_of(t * tile, tile), tile)
                    acc[at, :] += jnp.dot(weights, values, preferred_element_type=F32)
                    return 0

                lax.fori_loop(0, tiles, body, 0)

        if last:
            out = outs[r]
            bound = jnp.max(bound_in[r, 0, 0:8, :])
            for kp, vp in pieces:
                bound = jnp.maximum(bound, square_bound(kp[...]))
            q_most = jnp.max(bound_in[r, 0, 8:16, :])
            safe = bound * q_most <= (SAFE_LOG2 / EXP2_SCALE) ** 2

            @pl.when(safe)
            def _(acc=acc, out=out):
                for h in range(heads):
                    at = slice(h * rows, (h + 1) * rows)
                    out[:, h * HD : (h + 1) * HD] = (acc[at, :HD] / acc[at, HD:]).astype(BF16)

            @pl.when(jnp.logical_not(safe))
            def _(acc=acc, out=out, q_ref=q_ref, k_ref=k_ref, v_ref=v_ref, start=start, end=end):
                def absorb(h, keys, values, shown, fresh):
                    at = pl.ds(pl.multiple_of(h * rows, rows), rows)
                    q = q_ref[:, pl.ds(pl.multiple_of(h * HD, HD), HD)]
                    s = jnp.where(shown, scores_of(q, keys) * score_scale, masked_score)
                    most = jnp.max(s, axis=1, keepdims=True)
                    if fresh:
                        peak = jnp.broadcast_to(most, (rows, HD))
                    else:
                        before = peak_ref[at, :]
                        peak = jnp.maximum(before, most)
                    w = jnp.where(shown, jnp.exp(s - peak[:, :1]), 0.0)
                    total = jnp.broadcast_to(jnp.sum(w, axis=1, keepdims=True), (rows, HD))
                    gained = jnp.dot(w.astype(BF16), values, preferred_element_type=F32)
                    if not fresh:
                        factor = jnp.exp(before - peak)
                        total = total + total_ref[at, :] * factor
                        gained = gained + acc[at, 0:HD] * factor
                    peak_ref[at, :] = peak
                    total_ref[at, :] = total
                    acc[at, 0:HD] = gained

                def own(h, _):
                    absorb(h, k_ref[...], v_ref[...], causal_mask(rows), True)
                    return 0

                lax.fori_loop(0, heads, own, 0)
                for p, piece in enumerate(everything):
                    base = all_bases[p]
                    count = piece.shape[0]

                    @pl.when((base < end) & (base + count > start))
                    def _(piece=piece, base=base, count=count):
                        kcol = pl.multiple_of(kvh * HD, HD)
                        vcol = pl.multiple_of((HALF_KV + kvh) * HD, HD)
                        for col, buf in ((kcol, kbuf), (vcol, vbuf)):
                            copy = pltpu.make_async_copy(piece.at[:, pl.ds(col, HD)], buf, sem)
                            copy.start()
                            copy.wait()
                        token = base + lax.broadcasted_iota(jnp.int32, (rows, count), 1)
                        shown = (token >= start) & (token < end)

                        def body(h, _):
                            absorb(h, kbuf[...], vbuf[...], shown, False)
                            return 0

                        lax.fori_loop(0, heads, body, 0)

                def finish(h, _):
                    at = pl.ds(pl.multiple_of(h * rows, rows), rows)
                    out[:, pl.ds(pl.multiple_of(h * HD, HD), HD)] = (
                        acc[at, 0:HD] / total_ref[at, :]
                    ).astype(BF16)
                    return 0

                lax.fori_loop(0, heads, finish, 0)


def stage(doc_blocks, messages, pieces, state, everything=None, reader0=0, name="stage"):
    nr = len(messages)
    first = state is None
    last = everything is not None
    rows, width = messages[0].shape
    mine = width - (2 * HALF_KV + 1) * HD
    group = mine // HALF_KV
    heads = group // HD
    lead = mine // HD
    smem = pl.BlockSpec(memory_space=pltpu.SMEM)
    bases = jnp.stack([b for _, b in pieces]).astype(jnp.int32)
    args = [doc_blocks, bases]
    specs = [smem, smem]
    if last:
        args.append(jnp.stack([b for _, b in everything]).astype(jnp.int32))
        specs.append(smem)
    for m in messages:
        args += [m] * 4
        specs += [
            pl.BlockSpec((rows, group), lambda k: (0, k)),
            pl.BlockSpec((rows, HD), lambda k: (0, lead + k)),
            pl.BlockSpec((rows, HD), lambda k: (0, lead + HALF_KV + k)),
            pl.BlockSpec((rows, HD), lambda k: (0, lead + 2 * HALF_KV)),
        ]
    for a, _ in pieces:
        args += [a, a]
        specs += [
            pl.BlockSpec((a.shape[0], HD), lambda k: (0, k)),
            pl.BlockSpec((a.shape[0], HD), lambda k: (0, HALF_KV + k)),
        ]
    acc_shape = (2 if not last else nr, HALF_KV, heads * rows, 2 * HD)
    acc_spec = pl.BlockSpec((nr, 1, heads * rows, 2 * HD), lambda k: (reader0, k, 0, 0))
    bound_spec = pl.BlockSpec((nr, 1, 16, HD), lambda k: (reader0, k, 0, 0))
    if not first:
        args += list(state)
        specs += [acc_spec, bound_spec]
    scratch = []
    if last:
        args += [a for a, _ in everything]
        specs += [pl.BlockSpec(memory_space=pl.ANY)] * len(everything)
        count = everything[0][0].shape[0]
        out_shape = [jax.ShapeDtypeStruct((rows, mine), BF16)] * nr
        out_specs = [pl.BlockSpec((rows, group), lambda k: (0, k))] * nr
        scratch = [
            pltpu.VMEM((nr, 1, heads * rows, 2 * HD), F32),
            pltpu.VMEM((count, HD), BF16),
            pltpu.VMEM((count, HD), BF16),
            pltpu.VMEM((heads * rows, HD), F32),
            pltpu.VMEM((heads * rows, HD), F32),
            pltpu.SemaphoreType.DMA,
        ]
    else:
        out_shape = [
            jax.ShapeDtypeStruct(acc_shape, F32),
            jax.ShapeDtypeStruct((nr, HALF_KV, 16, HD), F32),
        ]
        out_specs = [acc_spec, bound_spec]
    keys = sum(a.shape[0] for a, _ in pieces)
    return pl.pallas_call(
        functools.partial(stage_kernel, nr, len(pieces), first, last, len(everything or ())),
        grid=(HALF_KV,),
        in_specs=specs,
        out_specs=out_specs,
        out_shape=out_shape,
        scratch_shapes=scratch,
        compiler_params=pltpu.CompilerParams(vmem_limit_bytes=VMEM),
        cost_estimate=pl.CostEstimate(
            flops=int(nr * HALF_KV * heads * rows * keys * HD * 2),
            bytes_accessed=8 << 20,
            transcendentals=0,
        ),
        name=name,
    )(*args)


def shards(
    prompt_queries,
    prompt_keys,
    prompt_values,
    cache_keys,
    cache_values,
    doc_blocks,
    reader_docs,
    reader_offsets,
):
    size = lax.axis_size("docs")
    me = lax.axis_index("docs").astype(jnp.int32)
    tokens = cache_keys.shape[0]
    half = lax.rem(me, 2)
    upper = lax.rem(me // 2, 2)

    def moved(x, pairs):
        return lax.ppermute(
            x, "docs", [(i, j) for i, j in pairs if 0 <= i < size and 0 <= j < size]
        )

    everyone = range(size)
    beside = lambda x: moved(x, [(i, i ^ 1) for i in everyone])
    across = lambda x: moved(x, [(i, i ^ 2) for i in everyone])
    onward = lambda x: moved(x, [(i, i + 4) for i in everyone])
    back = lambda x: moved(x, [(i, i - 4) for i in everyone])
    relay = lambda x: moved(x, [(i, i + 4 if (i // 2) % 2 == 0 else i - 4) for i in everyone])

    block_c, block_s = angle_rows(np.arange(COARSE) * BLK, attention_gain)
    coarse_c, coarse_s = angle_rows(np.arange(COARSE) * COARSE, attention_gain)
    token_c, token_s = angle_rows(np.arange(max(prompt_queries.shape[0], COARSE)), 1.0)
    cache_tables = [jnp.asarray(t) for t in (block_c, block_s, token_c[:BLK], token_s[:BLK])]
    query_tables = [jnp.asarray(t) for t in (coarse_c, coarse_s, token_c, token_s)]

    ids = jnp.stack([half, me * (tokens // BLK)])
    mine, theirs = prepare_cache(ids, doc_blocks, cache_tables, cache_keys, cache_values)
    other = beside(theirs)
    across_a = across(mine)
    prepared = [
        prepare_queries(
            w[None], reader_offsets, reader_docs, query_tables, prompt_queries, prompt_keys, prompt_values
        )
        for w in (half, 1 - half)
    ]
    own_message = prepared[0]
    side_message = beside(prepared[1])
    onward_b = onward(other)
    back_b = back(other)
    onward_a = onward(mine)
    back_a = back(mine)
    across_b = across(other)

    at = lambda chunk: chunk * tokens
    near = [(mine, at(me)), (other, at(me ^ 1))]
    state = stage(doc_blocks, [own_message, side_message], near, None, name="near")

    far_a = relay(across_a)
    far_b = across(jnp.where(upper == 0, back_b, onward_b))
    middle = [
        (across_a, at(me ^ 2)),
        (across_b, at(me ^ 3)),
        (onward_a, at(me - 4)),
        (onward_b, at((me - 4) ^ 1)),
        (back_a, at(me + 4)),
        (back_b, at((me + 4) ^ 1)),
    ]
    state = stage(doc_blocks, [own_message, side_message], middle, state, name="middle")

    partner = jnp.where(upper == 0, me - 4, me + 4) ^ 2
    far = [(far_a, at(partner)), (far_b, at(partner ^ 1))]
    everything = near + middle + far
    (side_out,) = stage(doc_blocks, [side_message], far, state, everything, 1, name="far_side")
    (own_out,) = stage(doc_blocks, [own_message], far, state, everything, 0, name="far_own")
    side_out = beside(side_out)
    low = jnp.where(half == 0, own_out, side_out)
    high = jnp.where(half == 0, side_out, own_out)
    return jnp.concatenate([low, high], axis=1)


def solution(mesh):
    both = P(("groups", "docs"))
    wide = P(("groups", "docs"), None)
    placed = (wide, wide, wide, wide, wide, P("groups"), both, both)
    return jax.shard_map(shards, mesh=mesh, in_specs=placed, out_specs=wide, check_vma=False)
```

```python
import functools
import math

import jax
import jax.numpy as jnp
import numpy as np
from jax import lax
from jax.experimental import pallas as pl
from jax.experimental.pallas import tpu as pltpu
from jax.sharding import PartitionSpec as P

HD = 128
BLK = 32
HALF_KV = 2
F32 = jnp.float32
BF16 = jnp.bfloat16

rope_base = 1000000.0
yarn_factor = 4.0
pretrain_context = 32768.0
beta_fast = 32.0
beta_slow = 1.0
attention_gain = 0.1 * math.log(4.0) + 1.0
score_scale = 1.0 / math.sqrt(HD)
EXP2_SCALE = score_scale * math.log2(math.e)
SAFE_LOG2 = 60.0
masked_score = -1e30
ROW_TILE_HEADS = 4
VMEM = 56 * 1024 * 1024


def yarn_table():
    half = HD // 2

    def correction(turns):
        return (
            HD * math.log(pretrain_context / (turns * 2.0 * math.pi)) / (2.0 * math.log(rope_base))
        )

    lower = max(math.floor(correction(beta_fast)), 0)
    upper = min(math.ceil(correction(beta_slow)), HD - 1)
    span_width = max(upper - lower, 0.001)
    table = []
    for column in range(half):
        base_freq = rope_base ** (-2.0 * column / HD)
        fraction = min(max((column - lower) / span_width, 0.0), 1.0)
        table.append(base_freq * fraction / yarn_factor + base_freq * (1.0 - fraction))
    return np.asarray(table, np.float32).astype(np.float64)


def angle_rows(positions, gain):
    angles = np.asarray(positions, np.float64)[:, None] * yarn_table()[None, :]
    cosine = np.cos(angles) * gain
    sine = np.sin(angles) * gain
    return (
        np.concatenate([cosine, cosine], axis=1).astype(np.float32),
        np.concatenate([-sine, sine], axis=1).astype(np.float32),
    )


COARSE = 64


def cache_kernel(ids, doc_blocks, table, k_ref, v_ref, mine_ref, theirs_ref):
    half = ids[0]
    first_block = ids[1]
    ndoc = doc_blocks.shape[0]
    width = HALF_KV * HD
    step = pl.program_id(0)
    blocks = k_ref.shape[0] // BLK
    c2 = table[2 * COARSE : 2 * COARSE + BLK, :]
    s2 = table[2 * COARSE + BLK : 2 * COARSE + 2 * BLK, :]
    for b in range(blocks):
        block = first_block + step * blocks + b

        def find(d, carry):
            start, begin = carry
            end = start + doc_blocks[d]
            return (end, jnp.where(start <= block, start, begin))

        _, begin = lax.fori_loop(0, ndoc, find, (jnp.int32(0), jnp.int32(0)), unroll=True)
        place = jnp.clip(block - begin, 0, COARSE - 1)
        c1 = table[pl.ds(place, 1), :]
        s1 = table[pl.ds(place + COARSE, 1), :]
        cosine = c1 * c2 - s1 * s2
        sine = s1 * c2 + c1 * s2
        rows = pl.ds(b * BLK, BLK)
        for out, which in ((mine_ref, half), (theirs_ref, 1 - half)):
            for j in range(HALF_KV):
                col = pl.multiple_of(which * width + j * HD, HD)
                x = k_ref[rows, pl.ds(col, HD)].astype(F32)
                y = x * cosine + pltpu.roll(x, HD // 2, 1) * sine
                out[rows, pl.ds(j * HD, HD)] = y.astype(BF16)
    for out, which in ((mine_ref, half), (theirs_ref, 1 - half)):
        col = pl.multiple_of(which * width, HD)
        out[:, pl.ds(width, width)] = v_ref[:, pl.ds(col, width)]


def prepare_cache(ids, doc_blocks, table, keys, values):
    tokens, columns = keys.shape
    steps = 2
    whole = lambda shape: pl.BlockSpec(shape, lambda i, *_: (0, 0))
    part = pl.BlockSpec((tokens // steps, columns), lambda i, *_: (i, 0))
    out = pl.BlockSpec((tokens // steps, columns), lambda i, *_: (i, 0))
    return pl.pallas_call(
        cache_kernel,
        grid_spec=pltpu.PrefetchScalarGridSpec(
            num_scalar_prefetch=2,
            grid=(steps,),
            in_specs=[whole(table.shape), part, part],
            out_specs=[out, out],
        ),
        out_shape=[jax.ShapeDtypeStruct((tokens, columns), BF16)] * 2,
        cost_estimate=pl.CostEstimate(flops=4000000, bytes_accessed=4 << 20, transcendentals=0),
        name="prepare_cache",
    )(ids, doc_blocks, table, keys, values)


def scores_of(q, k):
    return lax.dot_general(q, k, (((1,), (1,)), ((), ())), preferred_element_type=F32)


def square_bound(x):
    x = x.astype(F32)
    sums = jnp.dot((x * x).astype(BF16), jnp.ones((HD, HD), BF16), preferred_element_type=F32)
    return jnp.max(sums.reshape(-1, 8, HD), axis=0)


def span_of(doc_blocks, doc):
    def find(d, carry):
        total, start, end = carry
        size = doc_blocks[d]
        start = jnp.where(d == doc, total, start)
        end = jnp.where(d == doc, total + size, end)
        return (total + size, start, end)

    zero = jnp.int32(0)
    _, start, end = lax.fori_loop(0, doc_blocks.shape[0], find, (zero, zero, zero), unroll=True)
    return start * BLK, end * BLK


def causal_mask(n):
    return lax.broadcasted_iota(jnp.int32, (n, n), 1) <= lax.broadcasted_iota(jnp.int32, (n, n), 0)


def whole_number(ref, place):
    return jnp.max(ref[16 * place : 16 * place + 16, :].astype(F32)).astype(jnp.int32)


def turning(table, offset_hi, offset_lo, rows):
    ca, sa = table[pl.ds(offset_hi, 1), :], table[pl.ds(offset_hi + COARSE, 1), :]
    cb = table[pl.ds(offset_lo + 2 * COARSE, 1), :]
    sb = table[pl.ds(offset_lo + 2 * COARSE + rows, 1), :]
    c1 = ca * cb - sa * sb
    s1 = sa * cb + ca * sb
    c2 = table[2 * COARSE : 2 * COARSE + rows, :]
    s2 = table[2 * COARSE + rows : 2 * COARSE + 2 * rows, :]
    return c1 * c2 - s1 * s2, s1 * c2 + c1 * s2


def stage_kernel(chunks, all_chunks, slots, count, first, last, reader0, *refs):
    refs = list(refs)
    take = lambda n: [refs.pop(0) for _ in range(n)]
    (ids,) = take(1)
    if first:
        doc_blocks, own_doc, own_offset, table = take(4)
        readers = [take(3) for _ in range(2)]
        (numbers,) = take(1)
    else:
        spans, q_ref, k_ref, v_ref = take(4)
    pieces = [take(2) for _ in chunks]
    if not first:
        acc_in, bound_in = take(2)
    if last:
        everything = take(len(slots))
        out, acc = take(2)
        most_ref, fetched_k, fetched_v, peak_ref, total_ref, sem = take(6)
    elif first:
        acc_ref, bound_ref, spans, q_ref, k_ref, v_ref = take(6)
    else:
        acc_ref, bound_ref = take(2)
    kbuf, vbuf = take(2)
    kvh = pl.program_id(0)
    reader = reader0 if last else pl.program_id(1)
    me = ids[2]
    if last:
        most = most_ref
    else:
        acc = acc_ref.at[0, 0]
        most = bound_ref.at[0, 0, 0:8]
    q_rows = q_ref.at[0, 0]
    k_own, v_own = k_ref.at[0, 0], v_ref.at[0, 0]
    rows = k_own.shape[0]
    heads = q_rows.shape[0] // rows
    tile = ROW_TILE_HEADS * rows
    tiles = heads // ROW_TILE_HEADS
    at = lambda t: slice(t * tile, (t + 1) * tile)

    if first:
        for r, (raw_q, raw_k, raw_v) in enumerate(readers):

            @pl.when(reader == r)
            def _(r=r, raw_q=raw_q, raw_k=raw_k, raw_v=raw_v):
                if r == 0:
                    document = own_doc[0]
                    offset = jnp.clip(own_offset[0], 0, COARSE * COARSE - 1)
                    hi = offset // COARSE
                    lo = offset - hi * COARSE
                else:
                    document, hi, lo = [whole_number(numbers, i) for i in range(3)]
                begin, finish = span_of(doc_blocks, document)
                spans[2 * r] = begin
                spans[2 * r + 1] = finish
                cosine, sine = turning(table, hi, lo, rows)

                def rotated(x):
                    x = x.astype(F32)
                    return (x * cosine + pltpu.roll(x, HD // 2, 1) * sine).astype(BF16)

                k_own[...] = rotated(raw_k[...])
                v_own[...] = raw_v[...]
                for h in range(heads):
                    q_rows[h * rows : (h + 1) * rows, :] = rotated(
                        raw_q[:, h * HD : (h + 1) * HD]
                    )

    start = spans[2 * reader]
    end = spans[2 * reader + 1]

    if first:
        mask = jnp.concatenate([causal_mask(rows)] * ROW_TILE_HEADS, axis=0)
        keys = k_own[...]
        values = jnp.concatenate([v_own[...], jnp.ones((rows, HD), BF16)], axis=1)
        q_most = jnp.zeros((8, HD), F32)
        for t in range(tiles):
            q = q_rows[at(t), :]
            weights = jnp.exp2(scores_of(q, keys) * EXP2_SCALE)
            weights = jnp.where(mask, weights, 0.0).astype(BF16)
            acc[at(t), :] = jnp.dot(weights, values, preferred_element_type=F32)
            q_most = jnp.maximum(q_most, square_bound(q))
        most[...] = square_bound(keys)
        bound_ref[0, 0, 8:16, :] = q_most
    elif last:
        most[...] = bound_in[0, 0, 0:8, :]
    else:
        bound_ref[...] = bound_in[...]

    filled = jnp.int32(0)
    for p in range(0, len(pieces), 2):
        bases = [chunks[p + i](me) * count for i in range(2)]
        lows = [jnp.maximum(base, start) for base in bases]
        shown = [
            jnp.maximum(jnp.minimum(base + count, end) - low, 0)
            for base, low in zip(bases, lows, strict=True)
        ]
        ahead = [jnp.where(bases[i] > bases[1 - i], shown[1 - i], 0) for i in range(2)]
        for i in range(2):

            @pl.when(shown[i] > 0)
            def _(piece=pieces[p + i], put=count + filled + ahead[i] + bases[i] - lows[i]):
                to = pl.ds(pl.multiple_of(put, BLK), count)
                kbuf[to, :] = piece[0][...]
                vbuf[to, 0:HD] = piece[1][...]
                vbuf[to, HD:] = jnp.ones((count, HD), BF16)

        filled = filled + shown[0] + shown[1]
    some = filled > 0

    @pl.when(some)
    def _():
        to = pl.ds(pl.multiple_of(count + filled, BLK), count)
        kbuf[to, :] = jnp.zeros((count, HD), BF16)
        vbuf[to, :] = jnp.zeros((count, 2 * HD), BF16)
        if not first:
            acc[...] = acc_in[0, 0]

    def attend(step, _):
        here = pl.ds(pl.multiple_of(count + step * count, BLK), count)
        keys = kbuf[here, :]
        values = vbuf[here, :]
        most[...] = jnp.maximum(most[...], square_bound(keys))
        for t in range(tiles):
            weights = jnp.exp2(scores_of(q_rows[at(t), :], keys) * EXP2_SCALE).astype(BF16)
            acc[at(t), :] += jnp.dot(weights, values, preferred_element_type=F32)
        return 0

    lax.fori_loop(0, (filled + count - 1) // count, attend, 0)
    if not first and not last:

        @pl.when(jnp.logical_not(some))
        def _():
            acc[...] = acc_in[0, 0]

    if last:
        q_most = jnp.max(bound_in[0, 0, 8:16, :])
        safe = jnp.max(most[...]) * q_most <= (SAFE_LOG2 / EXP2_SCALE) ** 2
        for wanted, sums in ((some, acc), (jnp.logical_not(some), acc_in.at[0, 0])):

            @pl.when(safe & wanted)
            def _(sums=sums):
                for h in range(heads):
                    mine = slice(h * rows, (h + 1) * rows)
                    out[:, h * HD : (h + 1) * HD] = (sums[mine, :HD] / sums[mine, HD:]).astype(
                        BF16
                    )

        @pl.when(jnp.logical_not(safe))
        def _():
            def absorb(h, keys, values, shown, fresh):
                mine = pl.ds(pl.multiple_of(h * rows, rows), rows)
                s = jnp.where(shown, scores_of(q_rows[mine, :], keys) * score_scale, masked_score)
                most_now = jnp.max(s, axis=1, keepdims=True)
                if fresh:
                    peak = jnp.broadcast_to(most_now, (rows, HD))
                else:
                    before = peak_ref[mine, :]
                    peak = jnp.maximum(before, most_now)
                w = jnp.where(shown, jnp.exp(s - peak[:, :1]), 0.0)
                total = jnp.broadcast_to(jnp.sum(w, axis=1, keepdims=True), (rows, HD))
                gained = jnp.dot(w.astype(BF16), values, preferred_element_type=F32)
                if not fresh:
                    factor = jnp.exp(before - peak)
                    total = total + total_ref[mine, :] * factor
                    gained = gained + acc[mine, 0:HD] * factor
                peak_ref[mine, :] = peak
                total_ref[mine, :] = total
                acc[mine, 0:HD] = gained

            def own(h, _):
                absorb(h, k_own[...], v_own[...], causal_mask(rows), True)
                return 0

            lax.fori_loop(0, heads, own, 0)
            for p, piece in enumerate(everything):
                base = all_chunks[p](me) * count
                piece = piece.at[slots[p] * count : (slots[p] + 1) * count]

                @pl.when((base < end) & (base + count > start))
                def _(piece=piece, base=base):
                    kcol = pl.multiple_of(kvh * HD, HD)
                    vcol = pl.multiple_of((HALF_KV + kvh) * HD, HD)
                    for col, buf in ((kcol, fetched_k), (vcol, fetched_v)):
                        copy = pltpu.make_async_copy(piece.at[:, pl.ds(col, HD)], buf, sem)
                        copy.start()
                        copy.wait()
                    token = base + lax.broadcasted_iota(jnp.int32, (rows, count), 1)
                    shown = (token >= start) & (token < end)

                    def body(h, _):
                        absorb(h, fetched_k[...], fetched_v[...], shown, False)
                        return 0

                    lax.fori_loop(0, heads, body, 0)

            def finish(h, _):
                mine = pl.ds(pl.multiple_of(h * rows, rows), rows)
                out[:, pl.ds(pl.multiple_of(h * HD, HD), HD)] = (
                    acc[mine, 0:HD] / total_ref[mine, :]
                ).astype(BF16)
                return 0

            lax.fori_loop(0, heads, finish, 0)


def stage(ids, inputs, pieces, state, kept, everything=None, reader=None, whole=False, name="stage"):
    first = state is None
    last = everything is not None
    smem = pl.BlockSpec(memory_space=pltpu.SMEM)
    count = kept["count"]
    rows, heads = kept["rows"], kept["heads"]
    reader0 = reader or 0
    by = lambda k, r: (reader0, k, 0, 0) if last else (r, k, 0, 0)
    place = (lambda k, ids: by(k, 0)) if last else (lambda k, r, ids: by(k, r))
    head = lambda col, part=0: (
        (lambda k, ids: (part, col + k)) if last else (lambda k, r, ids: (part, col + k))
    )
    block = lambda *shape: pl.BlockSpec((1, 1) + shape, place)
    args = [ids]
    specs = []
    for a, spec in inputs:
        args.append(a)
        specs.append(smem if spec is None else spec)
    if not first:
        args += [kept["spans"], kept["q"], kept["k"], kept["v"]]
        specs += [smem, block(heads * rows, HD), block(rows, HD), block(rows, HD)]
    for a, part, _ in pieces:
        args += [a, a]
        specs += [
            pl.BlockSpec((count, HD), head(0, part)),
            pl.BlockSpec((count, HD), head(HALF_KV, part)),
        ]
    acc_spec = block(heads * rows, 2 * HD)
    bound_spec = block(16, HD)
    if not first:
        args += list(state)
        specs += [acc_spec, bound_spec]
    slots = []
    scratch = []
    if last:
        args += [a for a, _, _ in everything]
        specs += [pl.BlockSpec(memory_space=pl.ANY)] * len(everything)
        slots = [part for _, part, _ in everything]
        group = heads * HD
        columns = group * HALF_KV
        if whole:
            out_shape = [jax.ShapeDtypeStruct((rows, 2 * columns), BF16)]
            out_specs = [pl.BlockSpec((rows, group), lambda k, ids: (0, ids[0] * HALF_KV + k))]
        else:
            out_shape = [jax.ShapeDtypeStruct((rows, columns), BF16)]
            out_specs = [pl.BlockSpec((rows, group), lambda k, ids: (0, k))]
        scratch = [
            pltpu.VMEM((heads * rows, 2 * HD), F32),
            pltpu.VMEM((8, HD), F32),
            pltpu.VMEM((count, HD), BF16),
            pltpu.VMEM((count, HD), BF16),
            pltpu.VMEM((heads * rows, HD), F32),
            pltpu.VMEM((heads * rows, HD), F32),
            pltpu.SemaphoreType.DMA,
        ]
    else:
        full = lambda *shape: (2, HALF_KV) + shape
        out_shape = [
            jax.ShapeDtypeStruct(full(heads * rows, 2 * HD), F32),
            jax.ShapeDtypeStruct(full(16, HD), F32),
        ]
        out_specs = [acc_spec, bound_spec]
        if first:
            out_shape += [
                jax.ShapeDtypeStruct((4,), jnp.int32),
                jax.ShapeDtypeStruct(full(heads * rows, HD), BF16),
                jax.ShapeDtypeStruct(full(rows, HD), BF16),
                jax.ShapeDtypeStruct(full(rows, HD), BF16),
            ]
            out_specs += [smem, block(heads * rows, HD), block(rows, HD), block(rows, HD)]
    scratch += [
        pltpu.VMEM(((len(pieces) + 2) * count, HD), BF16),
        pltpu.VMEM(((len(pieces) + 2) * count, 2 * HD), BF16),
    ]
    return pl.pallas_call(
        functools.partial(
            stage_kernel,
            [chunk for _, _, chunk in pieces],
            [chunk for _, _, chunk in everything or ()],
            slots,
            count,
            first,
            last,
            reader0,
        ),
        grid_spec=pltpu.PrefetchScalarGridSpec(
            num_scalar_prefetch=1,
            grid=(HALF_KV,) if last else (HALF_KV, 2),
            in_specs=specs,
            out_specs=out_specs,
            scratch_shapes=scratch,
        ),
        out_shape=out_shape,
        compiler_params=pltpu.CompilerParams(vmem_limit_bytes=VMEM),
        cost_estimate=pl.CostEstimate(
            flops=15000000000 if first else 10000000000,
            bytes_accessed=1 << 18,
            transcendentals=0,
        ),
        name=name,
    )(*args)


def shards(
    prompt_queries,
    prompt_keys,
    prompt_values,
    cache_keys,
    cache_values,
    doc_blocks,
    reader_docs,
    reader_offsets,
):
    size = lax.axis_size("docs")
    me = lax.axis_index("docs").astype(jnp.int32)
    tokens = cache_keys.shape[0]
    half = lax.rem(me, 2)

    def moved(x, pairs):
        return lax.ppermute(
            x, "docs", [(i, j) for i, j in pairs if 0 <= i < size and 0 <= j < size]
        )

    everyone = range(size)
    second = lambda i: (i // 2) % 2
    beside = lambda x: moved(x, [(i, i ^ 1) for i in everyone])
    across = lambda x: moved(x, [(i, i ^ 2) for i in everyone])
    across_other = lambda x: moved(x, [(i, i ^ 3) for i in everyone])
    onward = lambda x: moved(x, [(i, i + 4) for i in everyone])
    onward_other = lambda x: moved(x, [(i, (i + 4) ^ 1) for i in everyone])
    back = lambda x: moved(x, [(i, i - 4) for i in everyone])
    back_other = lambda x: moved(x, [(i, (i - 4) ^ 1) for i in everyone])
    next_other = lambda x: moved(
        x, [(i, (i + 2) ^ 1 if second(i) else (i - 2) ^ 1) for i in everyone]
    )
    relay = lambda x: moved(x, [(i, i - 4 if second(i) else i + 4) for i in everyone])

    rows = prompt_queries.shape[0]
    block_rows = angle_rows(np.arange(COARSE) * BLK, attention_gain)
    coarse_rows = angle_rows(np.arange(COARSE) * COARSE, attention_gain)
    cache_table = np.concatenate(block_rows + angle_rows(np.arange(BLK), 1.0))
    query_table = np.concatenate(coarse_rows + angle_rows(np.arange(rows), 1.0))

    ids = jnp.stack([half, me * (tokens // BLK), me])
    columns = prompt_queries.shape[1] // 2
    width = prompt_keys.shape[1] // 2
    cut = lambda x: lax.dynamic_slice_in_dim(x, (1 - half) * (x.shape[1] // 2), x.shape[1] // 2, 1)
    offset = reader_offsets[0]
    numbers = jnp.stack([reader_docs[0], offset // COARSE, lax.rem(offset, COARSE)])
    numbers = jnp.concatenate([numbers, jnp.zeros((rows // 16 - 3,), jnp.int32)])
    numbers = jnp.broadcast_to(jnp.repeat(numbers.astype(BF16), 16)[:, None], (rows, HD))
    mine, theirs = prepare_cache(
        ids, doc_blocks, jnp.asarray(cache_table), cache_keys, cache_values
    )
    _, prompt_queries, prompt_keys, prompt_values = lax.optimization_barrier(
        (mine, prompt_queries, prompt_keys, prompt_values)
    )
    message = jnp.concatenate(
        [cut(prompt_queries), cut(prompt_keys), cut(prompt_values), numbers], axis=1
    )
    side = beside(message)
    other = beside(theirs)
    across_a = across(mine)
    chip = jnp.concatenate([mine, other], axis=0)
    onward_c = onward(chip)
    back_c = back(chip)
    across_b = across_other(theirs)

    near = [(mine, 0, lambda i: i), (other, 0, lambda i: i ^ 1)]
    group = columns // HALF_KV
    lead = columns // HD
    mine_at = lambda k, r, ids: (0, ids[0] * HALF_KV + k)
    side_at = lambda shift: lambda k, r, ids: (0, shift + k)
    wide = lambda place: pl.BlockSpec((rows, group), place)
    thin = lambda place: pl.BlockSpec((rows, HD), place)
    table = jnp.asarray(query_table)
    inputs = [
        (doc_blocks, None),
        (reader_docs, None),
        (reader_offsets, None),
        (table, pl.BlockSpec(table.shape, lambda k, r, ids: (0, 0))),
        (prompt_queries, wide(mine_at)),
        (prompt_keys, thin(mine_at)),
        (prompt_values, thin(mine_at)),
        (side, wide(side_at(0))),
        (side, thin(side_at(lead))),
        (side, thin(side_at(lead + HALF_KV))),
        (side, thin(lambda k, r, ids: (0, lead + 2 * HALF_KV))),
    ]
    kept = {"count": tokens, "rows": rows, "heads": group // HD}
    acc, bound, spans, turned_q, turned_k, kept_v = stage(
        ids, inputs, near, None, kept, name="near"
    )
    bound, theirs, passing = lax.optimization_barrier((bound, theirs, across_a))
    far_a = relay(passing)
    far_b = next_other(theirs)
    kept.update(spans=spans, q=turned_q, k=turned_k, v=kept_v)
    middle = [
        (onward_c, 0, lambda i: i - 4),
        (onward_c, 1, lambda i: (i - 4) ^ 1),
        (across_a, 0, lambda i: i ^ 2),
        (across_b, 0, lambda i: i ^ 3),
        (back_c, 0, lambda i: i + 4),
        (back_c, 1, lambda i: (i + 4) ^ 1),
    ]
    state = stage(ids, [], middle, (acc, bound), kept, name="middle")

    partner = lambda i: i - 2 + 4 * ((i >> 1) & 1)
    far = [(far_a, 0, partner), (far_b, 0, lambda i: partner(i) ^ 1)]
    everything = near + middle + far
    (side_out,) = stage(ids, [], far, state, kept, everything, 1, name="far_side")
    (own_out,) = stage(ids, [], far, state, kept, everything, 0, True, name="far_own")
    column = (1 - half) * side_out.shape[1]
    return lax.dynamic_update_slice(own_out, beside(side_out), (jnp.int32(0), column))


def solution(mesh):
    both = P(("groups", "docs"))
    wide = P(("groups", "docs"), None)
    placed = (wide, wide, wide, wide, wide, P("groups"), both, both)
    return jax.shard_map(shards, mesh=mesh, in_specs=placed, out_specs=wide, check_vma=False)
```

```python
import functools
import math

import jax
import jax.numpy as jnp
import numpy as np
from jax import lax
from jax.experimental import pallas as pl
from jax.experimental.pallas import tpu as pltpu
from jax.sharding import PartitionSpec as P

HD = 128
BLK = 32
HALF_KV = 2
F32 = jnp.float32
BF16 = jnp.bfloat16

rope_base = 1000000.0
yarn_factor = 4.0
pretrain_context = 32768.0
beta_fast = 32.0
beta_slow = 1.0
attention_gain = 0.1 * math.log(4.0) + 1.0
score_scale = 1.0 / math.sqrt(HD)
EXP2_SCALE = score_scale * math.log2(math.e)
SAFE_LOG2 = 60.0
masked_score = -1e30
ROW_TILE_HEADS = 4
VMEM = 28 * 1024 * 1024


def yarn_table():
    half = HD // 2

    def correction(turns):
        return (
            HD * math.log(pretrain_context / (turns * 2.0 * math.pi)) / (2.0 * math.log(rope_base))
        )

    lower = max(math.floor(correction(beta_fast)), 0)
    upper = min(math.ceil(correction(beta_slow)), HD - 1)
    span_width = max(upper - lower, 0.001)
    table = []
    for column in range(half):
        base_freq = rope_base ** (-2.0 * column / HD)
        fraction = min(max((column - lower) / span_width, 0.0), 1.0)
        table.append(base_freq * fraction / yarn_factor + base_freq * (1.0 - fraction))
    return np.asarray(table, np.float32).astype(np.float64)


def angle_rows(positions, gain):
    angles = np.asarray(positions, np.float64)[:, None] * yarn_table()[None, :]
    cosine = np.cos(angles) * gain
    sine = np.sin(angles) * gain
    return (
        np.concatenate([cosine, cosine], axis=1).astype(np.float32),
        np.concatenate([-sine, sine], axis=1).astype(np.float32),
    )


COARSE = 64


def cache_kernel(ids, doc_blocks, table, k_ref, v_ref, mine_ref, theirs_ref):
    half = ids[0]
    first_block = ids[1]
    ndoc = doc_blocks.shape[0]
    width = HALF_KV * HD
    step = pl.program_id(0)
    blocks = k_ref.shape[0] // BLK
    c2 = table[2 * COARSE : 2 * COARSE + BLK, :]
    s2 = table[2 * COARSE + BLK : 2 * COARSE + 2 * BLK, :]
    for b in range(blocks):
        block = first_block + step * blocks + b

        def find(d, carry):
            start, begin = carry
            end = start + doc_blocks[d]
            return (end, jnp.where(start <= block, start, begin))

        _, begin = lax.fori_loop(0, ndoc, find, (jnp.int32(0), jnp.int32(0)), unroll=True)
        place = jnp.clip(block - begin, 0, COARSE - 1)
        c1 = table[pl.ds(place, 1), :]
        s1 = table[pl.ds(place + COARSE, 1), :]
        cosine = c1 * c2 - s1 * s2
        sine = s1 * c2 + c1 * s2
        rows = pl.ds(b * BLK, BLK)
        for out, which in ((mine_ref, half), (theirs_ref, 1 - half)):
            for j in range(HALF_KV):
                col = pl.multiple_of(which * width + j * HD, HD)
                x = k_ref[rows, pl.ds(col, HD)].astype(F32)
                y = x * cosine + pltpu.roll(x, HD // 2, 1) * sine
                out[rows, pl.ds(j * HD, HD)] = y.astype(BF16)
    for out, which in ((mine_ref, half), (theirs_ref, 1 - half)):
        col = pl.multiple_of(which * width, HD)
        out[:, pl.ds(width, width)] = v_ref[:, pl.ds(col, width)]


def prepare_cache(ids, doc_blocks, table, keys, values):
    tokens, columns = keys.shape
    steps = 2
    whole = lambda shape: pl.BlockSpec(shape, lambda i, *_: (0, 0))
    part = pl.BlockSpec((tokens // steps, columns), lambda i, *_: (i, 0))
    out = pl.BlockSpec((tokens // steps, columns), lambda i, *_: (i, 0))
    return pl.pallas_call(
        cache_kernel,
        grid_spec=pltpu.PrefetchScalarGridSpec(
            num_scalar_prefetch=2,
            grid=(steps,),
            in_specs=[whole(table.shape), part, part],
            out_specs=[out, out],
        ),
        out_shape=[jax.ShapeDtypeStruct((tokens, columns), BF16)] * 2,
        cost_estimate=pl.CostEstimate(flops=4000000, bytes_accessed=4 << 20, transcendentals=0),
        name="prepare_cache",
    )(ids, doc_blocks, table, keys, values)


def scores_of(q, k):
    return lax.dot_general(q, k, (((1,), (1,)), ((), ())), preferred_element_type=F32)


def square_bound(x):
    sums = jnp.dot(x * x, jnp.ones((HD, HD), BF16), preferred_element_type=F32)
    return jnp.max(sums.reshape(-1, 8, HD), axis=0)


def span_of(doc_blocks, doc):
    def find(d, carry):
        total, start, end = carry
        size = doc_blocks[d]
        start = jnp.where(d == doc, total, start)
        end = jnp.where(d == doc, total + size, end)
        return (total + size, start, end)

    zero = jnp.int32(0)
    _, start, end = lax.fori_loop(0, doc_blocks.shape[0], find, (zero, zero, zero), unroll=True)
    return start * BLK, end * BLK


def causal_mask(n):
    return lax.broadcasted_iota(jnp.int32, (n, n), 1) <= lax.broadcasted_iota(jnp.int32, (n, n), 0)


def whole_number(ref, place):
    return jnp.max(ref[16 * place : 16 * place + 16].astype(F32)).astype(jnp.int32)


def turning(table, offset_hi, offset_lo, rows):
    ca, sa = table[pl.ds(offset_hi, 1), :], table[pl.ds(offset_hi + COARSE, 1), :]
    cb = table[pl.ds(offset_lo + 2 * COARSE, 1), :]
    sb = table[pl.ds(offset_lo + 2 * COARSE + rows, 1), :]
    c1 = ca * cb - sa * sb
    s1 = sa * cb + ca * sb
    c2 = table[2 * COARSE : 2 * COARSE + rows, :]
    s2 = table[2 * COARSE + rows : 2 * COARSE + 2 * rows, :]
    return c1 * c2 - s1 * s2, s1 * c2 + c1 * s2


def stage_kernel(chunks, all_chunks, slots, count, first, last, reader0, *refs):
    refs = list(refs)
    take = lambda n: [refs.pop(0) for _ in range(n)]
    (ids,) = take(1)
    if first:
        doc_blocks, own_doc, own_offset, table, *own_reader, side = take(8)
    else:
        spans, q_ref, k_ref, v_ref = take(4)
    pieces = take(len(slots))
    if not first:
        acc_in, bound_in = take(2)
    if last:
        out, acc_ref, bound_ref, peak_ref, total_ref = take(5)
    elif first:
        acc_ref, bound_ref, spans, q_ref, k_ref, v_ref = take(6)
    else:
        acc_ref, bound_ref = take(2)
    kbuf, vbuf = take(2)
    kvh = pl.program_id(0)
    reader = reader0 if last else pl.program_id(1)
    me = ids[2]
    acc = acc_ref.at[reader, kvh]
    most = bound_ref.at[reader, kvh, 0:8]
    q_rows = q_ref.at[reader, kvh]
    k_own, v_own = k_ref.at[reader, kvh], v_ref.at[reader, kvh]
    rows = k_own.shape[0]

    def part(p, col):
        place = pl.ds(pl.multiple_of((col + kvh) * HD, HD), HD)
        return pieces[p][slots[p] * count : (slots[p] + 1) * count, place]

    heads = q_rows.shape[0] // rows
    tile = ROW_TILE_HEADS * rows
    tiles = heads // ROW_TILE_HEADS
    at = lambda t: slice(t * tile, (t + 1) * tile)

    if first:
        lead = 2 * heads

        def side_part(col):
            return side[:, pl.ds(pl.multiple_of(col * HD, HD), HD)]

        for r in range(2):

            @pl.when(reader == r)
            def _(r=r):
                if r == 0:
                    document = own_doc[0]
                    offset = jnp.clip(own_offset[0], 0, COARSE * COARSE - 1)
                    hi = offset // COARSE
                    lo = offset - hi * COARSE
                    raw_q = lambda h: own_reader[0][:, h * HD : (h + 1) * HD]
                    raw_k, raw_v = own_reader[1][...], own_reader[2][...]
                else:
                    numbers = side_part(lead + 2 * HALF_KV)
                    document, hi, lo = [whole_number(numbers, i) for i in range(3)]
                    raw_q = lambda h: side_part(kvh * heads + h)
                    raw_k, raw_v = side_part(lead + kvh), side_part(lead + HALF_KV + kvh)
                begin, finish = span_of(doc_blocks, document)
                spans[2 * r] = begin
                spans[2 * r + 1] = finish
                cosine, sine = turning(table, hi, lo, rows)

                def rotated(x):
                    x = x.astype(F32)
                    return (x * cosine + pltpu.roll(x, HD // 2, 1) * sine).astype(BF16)

                k_own[...] = rotated(raw_k)
                v_own[...] = raw_v
                for h in range(heads):
                    q_rows[h * rows : (h + 1) * rows, :] = rotated(raw_q(h))

    start = spans[2 * reader]
    end = spans[2 * reader + 1]

    if first:
        mask = jnp.concatenate([causal_mask(rows)] * ROW_TILE_HEADS, axis=0)
        keys = k_own[...]
        values = jnp.concatenate([v_own[...], jnp.ones((rows, HD), BF16)], axis=1)
        q_most = jnp.zeros((8, HD), F32)
        for t in range(tiles):
            q = q_rows[at(t), :]
            weights = jnp.exp2(scores_of(q, keys) * EXP2_SCALE)
            weights = jnp.where(mask, weights, 0.0).astype(BF16)
            acc[at(t), :] = jnp.dot(weights, values, preferred_element_type=F32)
            q_most = jnp.maximum(q_most, square_bound(q))
        most[...] = square_bound(keys)
        bound_ref[reader, kvh, 8:16, :] = q_most

    filled = jnp.int32(0)
    for p in range(0, len(chunks), 2):
        bases = [chunks[p + i](me) * count for i in range(2)]
        lows = [jnp.maximum(base, start) for base in bases]
        shown = [
            jnp.maximum(jnp.minimum(base + count, end) - low, 0)
            for base, low in zip(bases, lows, strict=True)
        ]
        ahead = [jnp.where(bases[i] > bases[1 - i], shown[1 - i], 0) for i in range(2)]
        for i in range(2):

            @pl.when(shown[i] > 0)
            def _(p=p + i, put=count + filled + ahead[i] + bases[i] - lows[i]):
                to = pl.ds(pl.multiple_of(put, BLK), count)
                kbuf[to, :] = part(p, 0)
                vbuf[to, 0:HD] = part(p, HALF_KV)
                vbuf[to, HD:] = jnp.ones((count, HD), BF16)

        filled = filled + shown[0] + shown[1]
    some = filled > 0

    @pl.when(some)
    def _():
        to = pl.ds(pl.multiple_of(count + filled, BLK), count)
        kbuf[to, :] = jnp.zeros((count, HD), BF16)
        vbuf[to, :] = jnp.zeros((count, 2 * HD), BF16)

    def attend(step, _):
        here = pl.ds(pl.multiple_of(count + step * count, BLK), count)
        keys = kbuf[here, :]
        values = vbuf[here, :]
        most[...] = jnp.maximum(most[...], square_bound(keys))
        for t in range(tiles):
            weights = jnp.exp2(scores_of(q_rows[at(t), :], keys) * EXP2_SCALE).astype(BF16)
            acc[at(t), :] += jnp.dot(weights, values, preferred_element_type=F32)
        return 0

    lax.fori_loop(0, (filled + count - 1) // count, attend, 0)
    if last:
        q_most = jnp.max(bound_ref[reader, kvh, 8:16, :])
        safe = jnp.max(most[...]) * q_most <= (SAFE_LOG2 / EXP2_SCALE) ** 2

        @pl.when(safe)
        def _():
            for h in range(heads):
                mine = slice(h * rows, (h + 1) * rows)
                out[:, h * HD : (h + 1) * HD] = (acc[mine, :HD] / acc[mine, HD:]).astype(BF16)

        @pl.when(jnp.logical_not(safe))
        def _():
            def absorb(h, keys, values, shown, fresh):
                mine = pl.ds(pl.multiple_of(h * rows, rows), rows)
                s = jnp.where(shown, scores_of(q_rows[mine, :], keys) * score_scale, masked_score)
                most_now = jnp.max(s, axis=1, keepdims=True)
                if fresh:
                    peak = jnp.broadcast_to(most_now, (rows, HD))
                else:
                    before = peak_ref[mine, :]
                    peak = jnp.maximum(before, most_now)
                w = jnp.where(shown, jnp.exp(s - peak[:, :1]), 0.0)
                total = jnp.broadcast_to(jnp.sum(w, axis=1, keepdims=True), (rows, HD))
                gained = jnp.dot(w.astype(BF16), values, preferred_element_type=F32)
                if not fresh:
                    factor = jnp.exp(before - peak)
                    total = total + total_ref[mine, :] * factor
                    gained = gained + acc[mine, 0:HD] * factor
                peak_ref[mine, :] = peak
                total_ref[mine, :] = total
                acc[mine, 0:HD] = gained

            def own(h, _):
                absorb(h, k_own[...], v_own[...], causal_mask(rows), True)
                return 0

            lax.fori_loop(0, heads, own, 0)
            for p, chunk in enumerate(all_chunks):
                base = chunk(me) * count

                @pl.when((base < end) & (base + count > start))
                def _(p=p, base=base):
                    token = base + lax.broadcasted_iota(jnp.int32, (rows, count), 1)
                    shown = (token >= start) & (token < end)

                    def body(h, _):
                        absorb(h, part(p, 0), part(p, HALF_KV), shown, False)
                        return 0

                    lax.fori_loop(0, heads, body, 0)

            def finish(h, _):
                mine = pl.ds(pl.multiple_of(h * rows, rows), rows)
                out[:, pl.ds(pl.multiple_of(h * HD, HD), HD)] = (
                    acc[mine, 0:HD] / total_ref[mine, :]
                ).astype(BF16)
                return 0

            lax.fori_loop(0, heads, finish, 0)


def stage(ids, inputs, pieces_now, state, kept, everything=None, reader=0, whole=False, name="stage"):
    first = state is None
    last = everything is not None
    smem = pl.BlockSpec(memory_space=pltpu.SMEM)
    count = kept["count"]
    rows, heads = kept["rows"], kept["heads"]
    here = pl.BlockSpec(memory_space=pltpu.VMEM)
    pieces = everything or pieces_now
    args = [ids]
    specs = []
    for a, spec in inputs:
        args.append(a)
        specs.append(smem if spec == "scalar" else here if spec == "whole" else spec)
    if not first:
        args += [kept["spans"], kept["q"], kept["k"], kept["v"]]
        specs += [smem, here, here, here]
    args += [a for a, _, _ in pieces]
    specs += [here] * len(pieces)
    aliases = {}
    full = lambda *shape: (2, HALF_KV) + shape
    out_shape = [
        jax.ShapeDtypeStruct(full(heads * rows, 2 * HD), F32),
        jax.ShapeDtypeStruct(full(16, HD), F32),
    ]
    out_specs = [here, here]
    scratch = []
    if first:
        out_shape += [
            jax.ShapeDtypeStruct((4,), jnp.int32),
            jax.ShapeDtypeStruct(full(heads * rows, HD), BF16),
            jax.ShapeDtypeStruct(full(rows, HD), BF16),
            jax.ShapeDtypeStruct(full(rows, HD), BF16),
        ]
        out_specs += [smem, here, here, here]
    else:
        aliases = {len(args) + i: (1 if last else 0) + i for i in range(2)}
        args += list(state)
        specs += [here, here]
    if last:
        group = heads * HD
        columns = group * HALF_KV
        if whole:
            out_shape.insert(0, jax.ShapeDtypeStruct((rows, 2 * columns), BF16))
            out_specs.insert(
                0, pl.BlockSpec((rows, group), lambda k, ids: (0, ids[0] * HALF_KV + k))
            )
        else:
            out_shape.insert(0, jax.ShapeDtypeStruct((rows, columns), BF16))
            out_specs.insert(0, pl.BlockSpec((rows, group), lambda k, ids: (0, k)))
        scratch = [
            pltpu.VMEM((heads * rows, HD), F32),
            pltpu.VMEM((heads * rows, HD), F32),
        ]
    scratch += [
        pltpu.VMEM(((len(pieces_now) + 2) * count, HD), BF16),
        pltpu.VMEM(((len(pieces_now) + 2) * count, 2 * HD), BF16),
    ]
    return pl.pallas_call(
        functools.partial(
            stage_kernel,
            [chunk for _, _, chunk in pieces_now],
            [chunk for _, _, chunk in everything or ()],
            [part for _, part, _ in pieces],
            count,
            first,
            last,
            reader,
        ),
        grid_spec=pltpu.PrefetchScalarGridSpec(
            num_scalar_prefetch=1,
            grid=(HALF_KV,) if last else (HALF_KV, 2),
            in_specs=specs,
            out_specs=out_specs,
            scratch_shapes=scratch,
        ),
        out_shape=out_shape,
        input_output_aliases=aliases,
        compiler_params=pltpu.CompilerParams(vmem_limit_bytes=VMEM),
        cost_estimate=pl.CostEstimate(
            flops=15000000000 if first else 10000000000,
            bytes_accessed=1 << 18,
            transcendentals=0,
        ),
        name=name,
    )(*args)


def shards(
    prompt_queries,
    prompt_keys,
    prompt_values,
    cache_keys,
    cache_values,
    doc_blocks,
    reader_docs,
    reader_offsets,
):
    size = lax.axis_size("docs")
    me = lax.axis_index("docs").astype(jnp.int32)
    tokens = cache_keys.shape[0]
    half = lax.rem(me, 2)

    def moved(x, pairs):
        return lax.ppermute(
            x, "docs", [(i, j) for i, j in pairs if 0 <= i < size and 0 <= j < size]
        )

    everyone = range(size)
    second = lambda i: (i // 2) % 2
    beside = lambda x: moved(x, [(i, i ^ 1) for i in everyone])
    across = lambda x: moved(x, [(i, i ^ 2) for i in everyone])
    across_other = lambda x: moved(x, [(i, i ^ 3) for i in everyone])
    onward = lambda x: moved(x, [(i, i + 4) for i in everyone])
    onward_other = lambda x: moved(x, [(i, (i + 4) ^ 1) for i in everyone])
    back = lambda x: moved(x, [(i, i - 4) for i in everyone])
    back_other = lambda x: moved(x, [(i, (i - 4) ^ 1) for i in everyone])
    next_other = lambda x: moved(
        x, [(i, (i + 2) ^ 1 if second(i) else (i - 2) ^ 1) for i in everyone]
    )
    relay = lambda x: moved(x, [(i, i - 4 if second(i) else i + 4) for i in everyone])

    rows = prompt_queries.shape[0]
    block_rows = angle_rows(np.arange(COARSE) * BLK, attention_gain)
    coarse_rows = angle_rows(np.arange(COARSE) * COARSE, attention_gain)
    cache_table = np.concatenate(block_rows + angle_rows(np.arange(BLK), 1.0))
    query_table = np.concatenate(coarse_rows + angle_rows(np.arange(rows), 1.0))

    ids = jnp.stack([half, me * (tokens // BLK), me])
    columns = prompt_queries.shape[1] // 2
    width = prompt_keys.shape[1] // 2
    cut = lambda x: lax.dynamic_slice_in_dim(x, (1 - half) * (x.shape[1] // 2), x.shape[1] // 2, 1)
    offset = reader_offsets[0]
    numbers = jnp.stack([reader_docs[0], offset // COARSE, lax.rem(offset, COARSE)])
    numbers = jnp.concatenate([numbers, jnp.zeros((rows // 16 - 3,), jnp.int32)])
    numbers = jnp.broadcast_to(jnp.repeat(numbers.astype(BF16), 16)[:, None], (rows, HD))
    mine, theirs = prepare_cache(
        ids, doc_blocks, jnp.asarray(cache_table), cache_keys, cache_values
    )
    _, prompt_queries, prompt_keys, prompt_values = lax.optimization_barrier(
        (mine, prompt_queries, prompt_keys, prompt_values)
    )
    message = jnp.concatenate(
        [cut(prompt_queries), cut(prompt_keys), cut(prompt_values), numbers], axis=1
    )
    side = beside(message)
    other = beside(theirs)
    across_a = across(mine)
    chip = jnp.concatenate([mine, other], axis=0)
    onward_c = onward(chip)
    back_c = back(chip)
    across_b = across_other(theirs)

    near = [(mine, 0, lambda i: i), (other, 0, lambda i: i ^ 1)]
    group = columns // HALF_KV
    mine_at = lambda k, r, ids: (0, ids[0] * HALF_KV + k)
    wide = lambda place: pl.BlockSpec((rows, group), place)
    thin = lambda place: pl.BlockSpec((rows, HD), place)
    table = jnp.asarray(query_table)
    inputs = [
        (doc_blocks, "scalar"),
        (reader_docs, "scalar"),
        (reader_offsets, "scalar"),
        (table, "whole"),
        (prompt_queries, wide(mine_at)),
        (prompt_keys, thin(mine_at)),
        (prompt_values, thin(mine_at)),
        (side, "whole"),
    ]
    kept = {"count": tokens, "rows": rows, "heads": group // HD}
    acc, bound, spans, turned_q, turned_k, kept_v = stage(
        ids, inputs, near, None, kept, name="near"
    )
    bound, theirs, passing = lax.optimization_barrier((bound, theirs, across_a))
    far_a = relay(passing)
    far_b = next_other(theirs)
    kept.update(spans=spans, q=turned_q, k=turned_k, v=kept_v)
    middle = [
        (onward_c, 0, lambda i: i - 4),
        (onward_c, 1, lambda i: (i - 4) ^ 1),
        (across_a, 0, lambda i: i ^ 2),
        (across_b, 0, lambda i: i ^ 3),
        (back_c, 0, lambda i: i + 4),
        (back_c, 1, lambda i: (i + 4) ^ 1),
    ]
    state = stage(ids, [], middle, (acc, bound), kept, name="middle")

    partner = lambda i: i - 2 + 4 * ((i >> 1) & 1)
    far = [(far_a, 0, partner), (far_b, 0, lambda i: partner(i) ^ 1)]
    everything = far + near + middle
    side_out, *state = stage(ids, [], far, state, kept, everything, 1, name="far_side")
    own_out, *_ = stage(ids, [], far, state, kept, everything, 0, True, name="far_own")
    column = (1 - half) * side_out.shape[1]
    return lax.dynamic_update_slice(own_out, beside(side_out), (jnp.int32(0), column))


def solution(mesh):
    both = P(("groups", "docs"))
    wide = P(("groups", "docs"), None)
    placed = (wide, wide, wide, wide, wide, P("groups"), both, both)
    return jax.shard_map(shards, mesh=mesh, in_specs=placed, out_specs=wide, check_vma=False)
```

```python
import functools
import math

import jax
import jax.numpy as jnp
import numpy as np
from jax import lax
from jax.experimental import pallas as pl
from jax.experimental.pallas import tpu as pltpu
from jax.sharding import PartitionSpec as P

HD = 128
BLK = 32
HALF_KV = 2
F32 = jnp.float32
BF16 = jnp.bfloat16

rope_base = 1000000.0
yarn_factor = 4.0
pretrain_context = 32768.0
beta_fast = 32.0
beta_slow = 1.0
attention_gain = 0.1 * math.log(4.0) + 1.0
score_scale = 1.0 / math.sqrt(HD)
EXP2_SCALE = score_scale * math.log2(math.e)
SAFE_LOG2 = 60.0
masked_score = -1e30
ROW_TILE_HEADS = 4
VMEM = 28 * 1024 * 1024


def yarn_table():
    half = HD // 2

    def correction(turns):
        return (
            HD * math.log(pretrain_context / (turns * 2.0 * math.pi)) / (2.0 * math.log(rope_base))
        )

    lower = max(math.floor(correction(beta_fast)), 0)
    upper = min(math.ceil(correction(beta_slow)), HD - 1)
    span_width = max(upper - lower, 0.001)
    table = []
    for column in range(half):
        base_freq = rope_base ** (-2.0 * column / HD)
        fraction = min(max((column - lower) / span_width, 0.0), 1.0)
        table.append(base_freq * fraction / yarn_factor + base_freq * (1.0 - fraction))
    return np.asarray(table, np.float32).astype(np.float64)


def angle_rows(positions, gain):
    angles = np.asarray(positions, np.float64)[:, None] * yarn_table()[None, :]
    cosine = np.cos(angles) * gain
    sine = np.sin(angles) * gain
    return (
        np.concatenate([cosine, cosine], axis=1).astype(np.float32),
        np.concatenate([-sine, sine], axis=1).astype(np.float32),
    )


COARSE = 64


def cache_kernel(doc_blocks, table, k_ref, v_ref, mine_ref, theirs_ref):
    me = lax.axis_index("docs").astype(jnp.int32)
    half = lax.rem(me, 2)
    ndoc = doc_blocks.shape[0]
    width = HALF_KV * HD
    step = pl.program_id(0)
    blocks = k_ref.shape[0] // BLK
    first_block = me * blocks * pl.num_programs(0)
    c2 = table[2 * COARSE : 2 * COARSE + BLK, :]
    s2 = table[2 * COARSE + BLK : 2 * COARSE + 2 * BLK, :]
    for b in range(blocks):
        block = first_block + step * blocks + b

        def find(d, carry):
            start, begin = carry
            end = start + doc_blocks[d]
            return (end, jnp.where(start <= block, start, begin))

        _, begin = lax.fori_loop(0, ndoc, find, (jnp.int32(0), jnp.int32(0)), unroll=True)
        place = jnp.clip(block - begin, 0, COARSE - 1)
        c1 = table[pl.ds(place, 1), :]
        s1 = table[pl.ds(place + COARSE, 1), :]
        cosine = c1 * c2 - s1 * s2
        sine = s1 * c2 + c1 * s2
        rows = pl.ds(b * BLK, BLK)
        for out, which in ((mine_ref, half), (theirs_ref, 1 - half)):
            for j in range(HALF_KV):
                col = pl.multiple_of(which * width + j * HD, HD)
                x = k_ref[rows, pl.ds(col, HD)].astype(F32)
                y = x * cosine + pltpu.roll(x, HD // 2, 1) * sine
                out[rows, pl.ds(j * HD, HD)] = y.astype(BF16)
    for out, which in ((mine_ref, half), (theirs_ref, 1 - half)):
        col = pl.multiple_of(which * width, HD)
        out[:, pl.ds(width, width)] = v_ref[:, pl.ds(col, width)]


def prepare_cache(doc_blocks, table, keys, values):
    tokens, columns = keys.shape
    steps = 2
    whole = lambda shape: pl.BlockSpec(shape, lambda i, *_: (0, 0))
    part = pl.BlockSpec((tokens // steps, columns), lambda i, *_: (i, 0))
    out = pl.BlockSpec((tokens // steps, columns), lambda i, *_: (i, 0))
    return pl.pallas_call(
        cache_kernel,
        grid_spec=pltpu.PrefetchScalarGridSpec(
            num_scalar_prefetch=1,
            grid=(steps,),
            in_specs=[whole(table.shape), part, part],
            out_specs=[out, out],
        ),
        out_shape=[jax.ShapeDtypeStruct((tokens, columns), BF16)] * 2,
        cost_estimate=pl.CostEstimate(flops=4000000, bytes_accessed=4 << 20, transcendentals=0),
        name="prepare_cache",
    )(doc_blocks, table, keys, values)


def scores_of(q, k):
    return lax.dot_general(q, k, (((1,), (1,)), ((), ())), preferred_element_type=F32)


def square_bound(x):
    sums = jnp.dot(x * x, jnp.ones((HD, HD), BF16), preferred_element_type=F32)
    return jnp.max(sums.reshape(-1, 8, HD), axis=0)


def span_of(doc_blocks, doc):
    def find(d, carry):
        total, start, end = carry
        size = doc_blocks[d]
        start = jnp.where(d == doc, total, start)
        end = jnp.where(d == doc, total + size, end)
        return (total + size, start, end)

    zero = jnp.int32(0)
    _, start, end = lax.fori_loop(0, doc_blocks.shape[0], find, (zero, zero, zero), unroll=True)
    return start * BLK, end * BLK


def causal_mask(n):
    return lax.broadcasted_iota(jnp.int32, (n, n), 1) <= lax.broadcasted_iota(jnp.int32, (n, n), 0)


def whole_number(ref, place):
    return jnp.max(ref[16 * place : 16 * place + 16].astype(F32)).astype(jnp.int32)


def turning(table, offset_hi, offset_lo, rows):
    ca, sa = table[pl.ds(offset_hi, 1), :], table[pl.ds(offset_hi + COARSE, 1), :]
    cb = table[pl.ds(offset_lo + 2 * COARSE, 1), :]
    sb = table[pl.ds(offset_lo + 2 * COARSE + rows, 1), :]
    c1 = ca * cb - sa * sb
    s1 = sa * cb + ca * sb
    c2 = table[2 * COARSE : 2 * COARSE + rows, :]
    s2 = table[2 * COARSE + rows : 2 * COARSE + 2 * rows, :]
    return c1 * c2 - s1 * s2, s1 * c2 + c1 * s2


def stage_kernel(chunks, all_chunks, slots, count, first, last, head, *refs):
    refs = list(refs)
    take = lambda n: [refs.pop(0) for _ in range(n)]
    (ids,) = take(1)
    if first:
        doc_blocks, own_doc, own_offset, table, *own_reader, side = take(8)
    else:
        spans, q_ref, k_ref, v_ref = take(4)
    pieces = take(len(slots))
    if not first:
        acc_in, bound_in = take(2)
    if last:
        if head:
            take(1)
        own_out, side_out, acc_ref, bound_ref, out, peak_ref, total_ref = take(7)
    elif first:
        acc_ref, bound_ref, spans, q_ref, k_ref, v_ref = take(6)
    else:
        acc_ref, bound_ref = take(2)
    kbuf, vbuf = take(2)
    kvh = head if last else pl.program_id(0)
    reader = pl.program_id(0 if last else 1)
    me = ids[2]
    acc = acc_ref.at[reader, kvh]
    most = bound_ref.at[reader, kvh, 0:8]
    q_rows = q_ref.at[reader, kvh]
    k_own, v_own = k_ref.at[reader, kvh], v_ref.at[reader, kvh]
    rows = k_own.shape[0]

    def part(p, col):
        place = pl.ds(pl.multiple_of((col + kvh) * HD, HD), HD)
        return pieces[p][slots[p] * count : (slots[p] + 1) * count, place]

    heads = q_rows.shape[0] // rows
    tile = ROW_TILE_HEADS * rows
    tiles = heads // ROW_TILE_HEADS
    at = lambda t: slice(t * tile, (t + 1) * tile)

    if first:
        lead = 2 * heads

        def side_part(col):
            return side[:, pl.ds(pl.multiple_of(col * HD, HD), HD)]

        for r in range(2):

            @pl.when(reader == r)
            def _(r=r):
                if r == 0:
                    document = own_doc[0]
                    offset = jnp.clip(own_offset[0], 0, COARSE * COARSE - 1)
                    hi = offset // COARSE
                    lo = offset - hi * COARSE
                    raw_q = lambda h: own_reader[0][:, h * HD : (h + 1) * HD]
                    raw_k, raw_v = own_reader[1][...], own_reader[2][...]
                else:
                    numbers = side_part(lead + 2 * HALF_KV)
                    document, hi, lo = [whole_number(numbers, i) for i in range(3)]
                    raw_q = lambda h: side_part(kvh * heads + h)
                    raw_k, raw_v = side_part(lead + kvh), side_part(lead + HALF_KV + kvh)
                begin, finish = span_of(doc_blocks, document)
                spans[2 * r] = begin
                spans[2 * r + 1] = finish
                cosine, sine = turning(table, hi, lo, rows)

                def rotated(x):
                    x = x.astype(F32)
                    return (x * cosine + pltpu.roll(x, HD // 2, 1) * sine).astype(BF16)

                k_own[...] = rotated(raw_k)
                v_own[...] = raw_v
                for h in range(heads):
                    q_rows[h * rows : (h + 1) * rows, :] = rotated(raw_q(h))

    start = spans[2 * reader]
    end = spans[2 * reader + 1]

    if first:
        mask = jnp.concatenate([causal_mask(rows)] * ROW_TILE_HEADS, axis=0)
        keys = k_own[...]
        values = jnp.concatenate([v_own[...], jnp.ones((rows, HD), BF16)], axis=1)
        q_most = jnp.zeros((8, HD), F32)
        for t in range(tiles):
            q = q_rows[at(t), :]
            weights = jnp.exp2(scores_of(q, keys) * EXP2_SCALE)
            weights = jnp.where(mask, weights, 0.0).astype(BF16)
            acc[at(t), :] = jnp.dot(weights, values, preferred_element_type=F32)
            q_most = jnp.maximum(q_most, square_bound(q))
        most[...] = square_bound(keys)
        bound_ref[reader, kvh, 8:16, :] = q_most

    if not chunks:
        return
    filled = jnp.int32(0)
    for p in range(0, len(chunks), 2):
        bases = [chunks[p + i](me) * count for i in range(2)]
        lows = [jnp.maximum(base, start) for base in bases]
        shown = [
            jnp.maximum(jnp.minimum(base + count, end) - low, 0)
            for base, low in zip(bases, lows, strict=True)
        ]
        ahead = [jnp.where(bases[i] > bases[1 - i], shown[1 - i], 0) for i in range(2)]
        for i in range(2):

            @pl.when(shown[i] > 0)
            def _(p=p + i, put=count + filled + ahead[i] + bases[i] - lows[i]):
                to = pl.ds(pl.multiple_of(put, BLK), count)
                kbuf[to, :] = part(p, 0)
                vbuf[to, 0:HD] = part(p, HALF_KV)
                vbuf[to, HD:] = jnp.ones((count, HD), BF16)

        filled = filled + shown[0] + shown[1]
    some = filled > 0

    @pl.when(some)
    def _():
        to = pl.ds(pl.multiple_of(count + filled, BLK), count)
        kbuf[to, :] = jnp.zeros((count, HD), BF16)
        vbuf[to, :] = jnp.zeros((count, 2 * HD), BF16)

    def attend(step, _):
        here = pl.ds(pl.multiple_of(count + step * count, BLK), count)
        keys = kbuf[here, :]
        values = vbuf[here, :]
        most[...] = jnp.maximum(most[...], square_bound(keys))
        for t in range(tiles):
            weights = jnp.exp2(scores_of(q_rows[at(t), :], keys) * EXP2_SCALE).astype(BF16)
            acc[at(t), :] += jnp.dot(weights, values, preferred_element_type=F32)
        return 0

    lax.fori_loop(0, (filled + count - 1) // count, attend, 0)
    if last:
        q_most = jnp.max(bound_ref[reader, kvh, 8:16, :])
        safe = jnp.max(most[...]) * q_most <= (SAFE_LOG2 / EXP2_SCALE) ** 2

        @pl.when(safe)
        def _():
            for h in range(heads):
                mine = slice(h * rows, (h + 1) * rows)
                out[:, h * HD : (h + 1) * HD] = (acc[mine, :HD] / acc[mine, HD:]).astype(BF16)

        @pl.when(jnp.logical_not(safe))
        def _():
            def absorb(h, keys, values, shown, fresh):
                mine = pl.ds(pl.multiple_of(h * rows, rows), rows)
                s = jnp.where(shown, scores_of(q_rows[mine, :], keys) * score_scale, masked_score)
                most_now = jnp.max(s, axis=1, keepdims=True)
                if fresh:
                    peak = jnp.broadcast_to(most_now, (rows, HD))
                else:
                    before = peak_ref[mine, :]
                    peak = jnp.maximum(before, most_now)
                w = jnp.where(shown, jnp.exp(s - peak[:, :1]), 0.0)
                total = jnp.broadcast_to(jnp.sum(w, axis=1, keepdims=True), (rows, HD))
                gained = jnp.dot(w.astype(BF16), values, preferred_element_type=F32)
                if not fresh:
                    factor = jnp.exp(before - peak)
                    total = total + total_ref[mine, :] * factor
                    gained = gained + acc[mine, 0:HD] * factor
                peak_ref[mine, :] = peak
                total_ref[mine, :] = total
                acc[mine, 0:HD] = gained

            def own(h, _):
                absorb(h, k_own[...], v_own[...], causal_mask(rows), True)
                return 0

            lax.fori_loop(0, heads, own, 0)
            for p, chunk in enumerate(all_chunks):
                base = chunk(me) * count

                @pl.when((base < end) & (base + count > start))
                def _(p=p, base=base):
                    token = base + lax.broadcasted_iota(jnp.int32, (rows, count), 1)
                    shown = (token >= start) & (token < end)

                    def body(h, _):
                        absorb(h, part(p, 0), part(p, HALF_KV), shown, False)
                        return 0

                    lax.fori_loop(0, heads, body, 0)

            def finish(h, _):
                mine = pl.ds(pl.multiple_of(h * rows, rows), rows)
                out[:, pl.ds(pl.multiple_of(h * HD, HD), HD)] = (
                    acc[mine, 0:HD] / total_ref[mine, :]
                ).astype(BF16)
                return 0

            lax.fori_loop(0, heads, finish, 0)

        for r, done in enumerate((own_out, side_out)):

            @pl.when(reader == r)
            def _(done=done):
                done[...] = out[...]


def stage(ids, inputs, pieces_now, state, kept, everything=None, head=0, whole=None, name="stage"):
    first = state is None
    last = everything is not None
    smem = pl.BlockSpec(memory_space=pltpu.SMEM)
    count = kept["count"]
    rows, heads = kept["rows"], kept["heads"]
    here = pl.BlockSpec(memory_space=pltpu.VMEM)
    pieces = everything or pieces_now
    args = [ids]
    specs = []
    for a, spec in inputs:
        args.append(a)
        specs.append(smem if spec == "scalar" else here if spec == "whole" else spec)
    if not first:
        args += [kept["spans"], kept["q"], kept["k"], kept["v"]]
        specs += [smem, here, here, here]
    args += [a for a, _, _ in pieces]
    specs += [here] * len(pieces)
    aliases = {}
    full = lambda *shape: (2, HALF_KV) + shape
    out_shape = [
        jax.ShapeDtypeStruct(full(heads * rows, 2 * HD), F32),
        jax.ShapeDtypeStruct(full(16, HD), F32),
    ]
    out_specs = [here, here]
    scratch = []
    if first:
        out_shape += [
            jax.ShapeDtypeStruct((4,), jnp.int32),
            jax.ShapeDtypeStruct(full(heads * rows, HD), BF16),
            jax.ShapeDtypeStruct(full(rows, HD), BF16),
            jax.ShapeDtypeStruct(full(rows, HD), BF16),
        ]
        out_specs += [smem, here, here, here]
    else:
        aliases = {len(args) + i: (2 if last else 0) + i for i in range(2)}
        args += list(state)
        specs += [here, here]
    if last:
        group = heads * HD
        out_shape = [
            jax.ShapeDtypeStruct((rows, 2 * HALF_KV * group), BF16),
            jax.ShapeDtypeStruct((rows, group), BF16),
        ] + out_shape
        out_specs = [
            pl.BlockSpec((rows, group), lambda r, ids: (0, ids[0] * HALF_KV + head)),
            here,
        ] + out_specs
        if head:
            aliases[len(args)] = 0
            args.append(whole)
            specs.append(pl.BlockSpec(memory_space=pl.ANY))
        scratch = [
            pltpu.VMEM((rows, group), BF16),
            pltpu.VMEM((heads * rows, HD), F32),
            pltpu.VMEM((heads * rows, HD), F32),
        ]
    scratch += [
        pltpu.VMEM(((len(pieces_now) + 2) * count, HD), BF16),
        pltpu.VMEM(((len(pieces_now) + 2) * count, 2 * HD), BF16),
    ]
    return pl.pallas_call(
        functools.partial(
            stage_kernel,
            [chunk for _, _, chunk in pieces_now],
            [chunk for _, _, chunk in everything or ()],
            [part for _, part, _ in pieces],
            count,
            first,
            last,
            head,
        ),
        grid_spec=pltpu.PrefetchScalarGridSpec(
            num_scalar_prefetch=1,
            grid=(2,) if last else (HALF_KV, 2),
            in_specs=specs,
            out_specs=out_specs,
            scratch_shapes=scratch,
        ),
        out_shape=out_shape,
        input_output_aliases=aliases,
        compiler_params=pltpu.CompilerParams(vmem_limit_bytes=VMEM),
        cost_estimate=pl.CostEstimate(
            flops=15000000000 if first else 10000000000,
            bytes_accessed=1 << 18,
            transcendentals=0,
        ),
        name=name,
    )(*args)


def shards(
    prompt_queries,
    prompt_keys,
    prompt_values,
    cache_keys,
    cache_values,
    doc_blocks,
    reader_docs,
    reader_offsets,
):
    size = lax.axis_size("docs")
    me = lax.axis_index("docs").astype(jnp.int32)
    tokens = cache_keys.shape[0]
    half = lax.rem(me, 2)

    def moved(x, pairs):
        return lax.ppermute(
            x, "docs", [(i, j) for i, j in pairs if 0 <= i < size and 0 <= j < size]
        )

    everyone = range(size)
    second = lambda i: (i // 2) % 2
    beside = lambda x: moved(x, [(i, i ^ 1) for i in everyone])
    across = lambda x: moved(x, [(i, i ^ 2) for i in everyone])
    across_other = lambda x: moved(x, [(i, i ^ 3) for i in everyone])
    onward = lambda x: moved(x, [(i, i + 4) for i in everyone])
    onward_other = lambda x: moved(x, [(i, (i + 4) ^ 1) for i in everyone])
    back = lambda x: moved(x, [(i, i - 4) for i in everyone])
    back_other = lambda x: moved(x, [(i, (i - 4) ^ 1) for i in everyone])
    next_other = lambda x: moved(
        x, [(i, (i + 2) ^ 1 if second(i) else (i - 2) ^ 1) for i in everyone]
    )
    relay = lambda x: moved(x, [(i, i - 4 if second(i) else i + 4) for i in everyone])

    rows = prompt_queries.shape[0]
    block_rows = angle_rows(np.arange(COARSE) * BLK, attention_gain)
    coarse_rows = angle_rows(np.arange(COARSE) * COARSE, attention_gain)
    cache_table = np.concatenate(block_rows + angle_rows(np.arange(BLK), 1.0))
    query_table = np.concatenate(coarse_rows + angle_rows(np.arange(rows), 1.0))

    ids = jnp.stack([half, me * (tokens // BLK), me])
    columns = prompt_queries.shape[1] // 2
    width = prompt_keys.shape[1] // 2
    cut = lambda x: lax.dynamic_slice_in_dim(x, (1 - half) * (x.shape[1] // 2), x.shape[1] // 2, 1)
    offset = reader_offsets[0]
    numbers = jnp.stack([reader_docs[0], offset // COARSE, lax.rem(offset, COARSE)])
    numbers = jnp.concatenate([numbers, jnp.zeros((rows // 16 - 3,), jnp.int32)])
    numbers = jnp.broadcast_to(jnp.repeat(numbers.astype(BF16), 16)[:, None], (rows, HD))
    mine, theirs = prepare_cache(
        doc_blocks, jnp.asarray(cache_table), cache_keys, cache_values
    )
    _, prompt_queries, prompt_keys, prompt_values = lax.optimization_barrier(
        (mine, prompt_queries, prompt_keys, prompt_values)
    )
    message = jnp.concatenate(
        [cut(prompt_queries), cut(prompt_keys), cut(prompt_values), numbers], axis=1
    )
    side = beside(message)
    other = beside(theirs)
    across_a = across(mine)
    chip = jnp.concatenate([mine, other], axis=0)
    onward_c = onward(chip)
    back_c = back(chip)
    across_b = across_other(lax.optimization_barrier((theirs, chip))[0])

    near = [(mine, 0, lambda i: i), (other, 0, lambda i: i ^ 1)]
    group = columns // HALF_KV
    mine_at = lambda k, r, ids: (0, ids[0] * HALF_KV + k)
    wide = lambda place: pl.BlockSpec((rows, group), place)
    thin = lambda place: pl.BlockSpec((rows, HD), place)
    table = jnp.asarray(query_table)
    inputs = [
        (doc_blocks, "scalar"),
        (reader_docs, "scalar"),
        (reader_offsets, "scalar"),
        (table, "whole"),
        (prompt_queries, wide(mine_at)),
        (prompt_keys, thin(mine_at)),
        (prompt_values, thin(mine_at)),
        (side, "whole"),
    ]
    kept = {"count": tokens, "rows": rows, "heads": group // HD}
    acc, bound, spans, turned_q, turned_k, kept_v = stage(
        ids, inputs, [], None, kept, name="alone"
    )
    bound, theirs, passing = lax.optimization_barrier((bound, theirs, across_a))
    far_a = relay(passing)
    far_b = next_other(theirs)
    kept.update(spans=spans, q=turned_q, k=turned_k, v=kept_v)
    middle = [
        (onward_c, 0, lambda i: i - 4),
        (onward_c, 1, lambda i: (i - 4) ^ 1),
        (across_a, 0, lambda i: i ^ 2),
        (across_b, 0, lambda i: i ^ 3),
        (back_c, 0, lambda i: i + 4),
        (back_c, 1, lambda i: (i + 4) ^ 1),
    ]
    state = stage(ids, [], near, (acc, bound), kept, name="near")
    state = stage(ids, [], middle, state, kept, name="middle")

    partner = lambda i: i - 2 + 4 * ((i >> 1) & 1)
    far = [(far_a, 0, partner), (far_b, 0, lambda i: partner(i) ^ 1)]
    everything = far + near + middle
    whole, sides = None, []
    for head in range(HALF_KV):
        whole, side_out, *state = stage(
            ids, [], far, state, kept, everything, head, whole, name="far"
        )
        sides.append(beside(side_out))
    for head, came in enumerate(sides):
        column = (1 - half) * columns + head * group
        whole = lax.dynamic_update_slice(whole, came, (jnp.int32(0), column))
    return whole


def solution(mesh):
    both = P(("groups", "docs"))
    wide = P(("groups", "docs"), None)
    placed = (wide, wide, wide, wide, wide, P("groups"), both, both)
    return jax.shard_map(shards, mesh=mesh, in_specs=placed, out_specs=wide, check_vma=False)
```

```python
import functools
import math

import jax
import jax.numpy as jnp
import numpy as np
from jax import lax
from jax.experimental import pallas as pl
from jax.experimental.pallas import tpu as pltpu
from jax.sharding import PartitionSpec as P

HD = 128
BLK = 32
HALF_KV = 2
F32 = jnp.float32
BF16 = jnp.bfloat16

rope_base = 1000000.0
yarn_factor = 4.0
pretrain_context = 32768.0
beta_fast = 32.0
beta_slow = 1.0
attention_gain = 0.1 * math.log(4.0) + 1.0
score_scale = 1.0 / math.sqrt(HD)
EXP2_SCALE = score_scale * math.log2(math.e)
SAFE_LOG2 = 60.0
masked_score = -1e30
ROW_TILE_HEADS = 4
VMEM = 28 * 1024 * 1024


def yarn_table():
    half = HD // 2

    def correction(turns):
        return (
            HD * math.log(pretrain_context / (turns * 2.0 * math.pi)) / (2.0 * math.log(rope_base))
        )

    lower = max(math.floor(correction(beta_fast)), 0)
    upper = min(math.ceil(correction(beta_slow)), HD - 1)
    span_width = max(upper - lower, 0.001)
    table = []
    for column in range(half):
        base_freq = rope_base ** (-2.0 * column / HD)
        fraction = min(max((column - lower) / span_width, 0.0), 1.0)
        table.append(base_freq * fraction / yarn_factor + base_freq * (1.0 - fraction))
    return np.asarray(table, np.float32).astype(np.float64)


def angle_rows(positions, gain):
    angles = np.asarray(positions, np.float64)[:, None] * yarn_table()[None, :]
    cosine = np.cos(angles) * gain
    sine = np.sin(angles) * gain
    return (
        np.concatenate([cosine, cosine], axis=1).astype(np.float32),
        np.concatenate([-sine, sine], axis=1).astype(np.float32),
    )


COARSE = 64


def cache_kernel(
    doc_blocks,
    doc,
    offset,
    table,
    k_ref,
    v_ref,
    q_all,
    k_all,
    v_all,
    mine_ref,
    theirs_ref,
    message,
):
    me = lax.axis_index("docs").astype(jnp.int32)
    half = lax.rem(me, 2)
    ndoc = doc_blocks.shape[0]
    width = HALF_KV * HD
    step = pl.program_id(0)
    @pl.when(step == 0)
    def _():
        place = 0
        for ref in (q_all, k_all, v_all):
            size = ref.shape[1] // 2
            col = pl.multiple_of((1 - half) * size, HD)
            message[:, place : place + size] = ref[:, pl.ds(col, size)]
            place += size
        at = jnp.clip(offset[0], 0, COARSE * COARSE - 1)
        hi = at // COARSE
        shape = (message.shape[0], HD)
        row = lax.broadcasted_iota(jnp.int32, shape, 0) // 16
        value = jnp.where(row == 0, doc[0], jnp.where(row == 1, hi, at - hi * COARSE))
        message[:, place : place + HD] = value.astype(F32).astype(BF16)

    blocks = k_ref.shape[0] // BLK
    first_block = me * blocks * pl.num_programs(0)
    c2 = table[2 * COARSE : 2 * COARSE + BLK, :]
    s2 = table[2 * COARSE + BLK : 2 * COARSE + 2 * BLK, :]
    for b in range(blocks):
        block = first_block + step * blocks + b

        def find(d, carry):
            start, begin = carry
            end = start + doc_blocks[d]
            return (end, jnp.where(start <= block, start, begin))

        _, begin = lax.fori_loop(0, ndoc, find, (jnp.int32(0), jnp.int32(0)), unroll=True)
        place = jnp.clip(block - begin, 0, COARSE - 1)
        c1 = table[pl.ds(place, 1), :]
        s1 = table[pl.ds(place + COARSE, 1), :]
        cosine = c1 * c2 - s1 * s2
        sine = s1 * c2 + c1 * s2
        rows = pl.ds(b * BLK, BLK)
        for out, which in ((mine_ref, half), (theirs_ref, 1 - half)):
            for j in range(HALF_KV):
                col = pl.multiple_of(which * width + j * HD, HD)
                x = k_ref[rows, pl.ds(col, HD)].astype(F32)
                y = x * cosine + pltpu.roll(x, HD // 2, 1) * sine
                out[rows, pl.ds(j * HD, HD)] = y.astype(BF16)
    for out, which in ((mine_ref, half), (theirs_ref, 1 - half)):
        col = pl.multiple_of(which * width, HD)
        out[:, pl.ds(width, width)] = v_ref[:, pl.ds(col, width)]


def prepare_cache(doc_blocks, doc, offset, table, keys, values, prompt):
    tokens, columns = keys.shape
    rows = prompt[0].shape[0]
    wide = sum(a.shape[1] // 2 for a in prompt) + HD
    steps = 2
    whole = lambda shape: pl.BlockSpec(shape, lambda i, *_: (0, 0))
    part = pl.BlockSpec((tokens // steps, columns), lambda i, *_: (i, 0))
    out = pl.BlockSpec((tokens // steps, columns), lambda i, *_: (i, 0))
    return pl.pallas_call(
        cache_kernel,
        grid_spec=pltpu.PrefetchScalarGridSpec(
            num_scalar_prefetch=3,
            grid=(steps,),
            in_specs=[whole(table.shape), part, part] + [whole(a.shape) for a in prompt],
            out_specs=[out, out, whole((rows, wide))],
        ),
        out_shape=[jax.ShapeDtypeStruct((tokens, columns), BF16)] * 2
        + [jax.ShapeDtypeStruct((rows, wide), BF16)],
        cost_estimate=pl.CostEstimate(flops=4000000, bytes_accessed=4 << 20, transcendentals=0),
        name="prepare_cache",
    )(doc_blocks, doc, offset, table, keys, values, *prompt)


def scores_of(q, k):
    return lax.dot_general(q, k, (((1,), (1,)), ((), ())), preferred_element_type=F32)


def square_bound(x):
    sums = jnp.dot(x * x, jnp.ones((HD, HD), BF16), preferred_element_type=F32)
    return jnp.max(sums.reshape(-1, 8, HD), axis=0)


def span_of(doc_blocks, doc):
    def find(d, carry):
        total, start, end = carry
        size = doc_blocks[d]
        start = jnp.where(d == doc, total, start)
        end = jnp.where(d == doc, total + size, end)
        return (total + size, start, end)

    zero = jnp.int32(0)
    _, start, end = lax.fori_loop(0, doc_blocks.shape[0], find, (zero, zero, zero), unroll=True)
    return start * BLK, end * BLK


def causal_mask(n):
    return lax.broadcasted_iota(jnp.int32, (n, n), 1) <= lax.broadcasted_iota(jnp.int32, (n, n), 0)


def whole_number(ref, place):
    return jnp.max(ref[16 * place : 16 * place + 16].astype(F32)).astype(jnp.int32)


def turning(table, offset_hi, offset_lo, rows):
    ca, sa = table[pl.ds(offset_hi, 1), :], table[pl.ds(offset_hi + COARSE, 1), :]
    cb = table[pl.ds(offset_lo + 2 * COARSE, 1), :]
    sb = table[pl.ds(offset_lo + 2 * COARSE + rows, 1), :]
    c1 = ca * cb - sa * sb
    s1 = sa * cb + ca * sb
    c2 = table[2 * COARSE : 2 * COARSE + rows, :]
    s2 = table[2 * COARSE + rows : 2 * COARSE + 2 * rows, :]
    return c1 * c2 - s1 * s2, s1 * c2 + c1 * s2


def stage_kernel(chunks, all_chunks, slots, count, first, last, head, *refs):
    refs = list(refs)
    take = lambda n: [refs.pop(0) for _ in range(n)]
    (ids,) = take(1)
    if first:
        doc_blocks, own_doc, own_offset, table, *own_reader, side = take(8)
    else:
        spans, q_ref, k_ref, v_ref = take(4)
    pieces = take(len(slots))
    if not first:
        acc_in, bound_in = take(2)
    if last:
        if head:
            take(1)
        own_out, side_out, acc_ref, bound_ref, out, peak_ref, total_ref = take(7)
    elif first:
        acc_ref, bound_ref, spans, q_ref, k_ref, v_ref = take(6)
    else:
        acc_ref, bound_ref = take(2)
    kbuf, vbuf = take(2)
    kvh = head if last else pl.program_id(0)
    reader = pl.program_id(0 if last else 1)
    me = ids[2]
    acc = acc_ref.at[reader, kvh]
    most = bound_ref.at[reader, kvh, 0:8]
    q_rows = q_ref.at[reader, kvh]
    k_own, v_own = k_ref.at[reader, kvh], v_ref.at[reader, kvh]
    rows = k_own.shape[0]

    def part(p, col):
        place = pl.ds(pl.multiple_of((col + kvh) * HD, HD), HD)
        return pieces[p][slots[p] * count : (slots[p] + 1) * count, place]

    heads = q_rows.shape[0] // rows
    tile = ROW_TILE_HEADS * rows
    tiles = heads // ROW_TILE_HEADS
    at = lambda t: slice(t * tile, (t + 1) * tile)

    if first:
        lead = 2 * heads

        def side_part(col):
            return side[:, pl.ds(pl.multiple_of(col * HD, HD), HD)]

        for r in range(2):

            @pl.when(reader == r)
            def _(r=r):
                if r == 0:
                    document = own_doc[0]
                    offset = jnp.clip(own_offset[0], 0, COARSE * COARSE - 1)
                    hi = offset // COARSE
                    lo = offset - hi * COARSE
                    raw_q = lambda h: own_reader[0][:, h * HD : (h + 1) * HD]
                    raw_k, raw_v = own_reader[1][...], own_reader[2][...]
                else:
                    numbers = side_part(lead + 2 * HALF_KV)
                    document, hi, lo = [whole_number(numbers, i) for i in range(3)]
                    raw_q = lambda h: side_part(kvh * heads + h)
                    raw_k, raw_v = side_part(lead + kvh), side_part(lead + HALF_KV + kvh)
                begin, finish = span_of(doc_blocks, document)
                spans[2 * r] = begin
                spans[2 * r + 1] = finish
                cosine, sine = turning(table, hi, lo, rows)

                def rotated(x):
                    x = x.astype(F32)
                    return (x * cosine + pltpu.roll(x, HD // 2, 1) * sine).astype(BF16)

                k_own[...] = rotated(raw_k)
                v_own[...] = raw_v
                for h in range(heads):
                    q_rows[h * rows : (h + 1) * rows, :] = rotated(raw_q(h))

    start = spans[2 * reader]
    end = spans[2 * reader + 1]

    if first:
        mask = jnp.concatenate([causal_mask(rows)] * ROW_TILE_HEADS, axis=0)
        keys = k_own[...]
        values = jnp.concatenate([v_own[...], jnp.ones((rows, HD), BF16)], axis=1)
        q_most = jnp.zeros((8, HD), F32)
        for t in range(tiles):
            q = q_rows[at(t), :]
            weights = jnp.exp2(scores_of(q, keys) * EXP2_SCALE)
            weights = jnp.where(mask, weights, 0.0).astype(BF16)
            acc[at(t), :] = jnp.dot(weights, values, preferred_element_type=F32)
            q_most = jnp.maximum(q_most, square_bound(q))
        most[...] = square_bound(keys)
        bound_ref[reader, kvh, 8:16, :] = q_most

    if not chunks:
        return
    filled = jnp.int32(0)
    for p in range(0, len(chunks), 2):
        bases = [chunks[p + i](me) * count for i in range(2)]
        lows = [jnp.maximum(base, start) for base in bases]
        shown = [
            jnp.maximum(jnp.minimum(base + count, end) - low, 0)
            for base, low in zip(bases, lows, strict=True)
        ]
        ahead = [jnp.where(bases[i] > bases[1 - i], shown[1 - i], 0) for i in range(2)]
        for i in range(2):

            @pl.when(shown[i] > 0)
            def _(p=p + i, put=count + filled + ahead[i] + bases[i] - lows[i]):
                to = pl.ds(pl.multiple_of(put, BLK), count)
                kbuf[to, :] = part(p, 0)
                vbuf[to, 0:HD] = part(p, HALF_KV)
                vbuf[to, HD:] = jnp.ones((count, HD), BF16)

        filled = filled + shown[0] + shown[1]
    some = filled > 0

    @pl.when(some)
    def _():
        to = pl.ds(pl.multiple_of(count + filled, BLK), count)
        kbuf[to, :] = jnp.zeros((count, HD), BF16)
        vbuf[to, :] = jnp.zeros((count, 2 * HD), BF16)

    def attend(step, _):
        here = pl.ds(pl.multiple_of(count + step * count, BLK), count)
        keys = kbuf[here, :]
        values = vbuf[here, :]
        most[...] = jnp.maximum(most[...], square_bound(keys))
        for t in range(tiles):
            weights = jnp.exp2(scores_of(q_rows[at(t), :], keys) * EXP2_SCALE).astype(BF16)
            acc[at(t), :] += jnp.dot(weights, values, preferred_element_type=F32)
        return 0

    lax.fori_loop(0, (filled + count - 1) // count, attend, 0)
    if last:
        q_most = jnp.max(bound_ref[reader, kvh, 8:16, :])
        safe = jnp.max(most[...]) * q_most <= (SAFE_LOG2 / EXP2_SCALE) ** 2

        @pl.when(safe)
        def _():
            for h in range(heads):
                mine = slice(h * rows, (h + 1) * rows)
                out[:, h * HD : (h + 1) * HD] = (acc[mine, :HD] / acc[mine, HD:]).astype(BF16)

        @pl.when(jnp.logical_not(safe))
        def _():
            def absorb(h, keys, values, shown, fresh):
                mine = pl.ds(pl.multiple_of(h * rows, rows), rows)
                s = jnp.where(shown, scores_of(q_rows[mine, :], keys) * score_scale, masked_score)
                most_now = jnp.max(s, axis=1, keepdims=True)
                if fresh:
                    peak = jnp.broadcast_to(most_now, (rows, HD))
                else:
                    before = peak_ref[mine, :]
                    peak = jnp.maximum(before, most_now)
                w = jnp.where(shown, jnp.exp(s - peak[:, :1]), 0.0)
                total = jnp.broadcast_to(jnp.sum(w, axis=1, keepdims=True), (rows, HD))
                gained = jnp.dot(w.astype(BF16), values, preferred_element_type=F32)
                if not fresh:
                    factor = jnp.exp(before - peak)
                    total = total + total_ref[mine, :] * factor
                    gained = gained + acc[mine, 0:HD] * factor
                peak_ref[mine, :] = peak
                total_ref[mine, :] = total
                acc[mine, 0:HD] = gained

            def own(h, _):
                absorb(h, k_own[...], v_own[...], causal_mask(rows), True)
                return 0

            lax.fori_loop(0, heads, own, 0)
            for p, chunk in enumerate(all_chunks):
                base = chunk(me) * count

                @pl.when((base < end) & (base + count > start))
                def _(p=p, base=base):
                    token = base + lax.broadcasted_iota(jnp.int32, (rows, count), 1)
                    shown = (token >= start) & (token < end)

                    def body(h, _):
                        absorb(h, part(p, 0), part(p, HALF_KV), shown, False)
                        return 0

                    lax.fori_loop(0, heads, body, 0)

            def finish(h, _):
                mine = pl.ds(pl.multiple_of(h * rows, rows), rows)
                out[:, pl.ds(pl.multiple_of(h * HD, HD), HD)] = (
                    acc[mine, 0:HD] / total_ref[mine, :]
                ).astype(BF16)
                return 0

            lax.fori_loop(0, heads, finish, 0)

        for r, done in enumerate((own_out, side_out)):

            @pl.when(reader == r)
            def _(done=done):
                done[...] = out[...]


def stage(ids, inputs, pieces_now, state, kept, everything=None, head=0, whole=None, name="stage"):
    first = state is None
    last = everything is not None
    smem = pl.BlockSpec(memory_space=pltpu.SMEM)
    count = kept["count"]
    rows, heads = kept["rows"], kept["heads"]
    here = pl.BlockSpec(memory_space=pltpu.VMEM)
    pieces = everything or pieces_now
    args = [ids]
    specs = []
    for a, spec in inputs:
        args.append(a)
        specs.append(smem if spec == "scalar" else here if spec == "whole" else spec)
    if not first:
        args += [kept["spans"], kept["q"], kept["k"], kept["v"]]
        specs += [smem, here, here, here]
    args += [a for a, _, _ in pieces]
    specs += [here] * len(pieces)
    aliases = {}
    full = lambda *shape: (2, HALF_KV) + shape
    out_shape = [
        jax.ShapeDtypeStruct(full(heads * rows, 2 * HD), F32),
        jax.ShapeDtypeStruct(full(16, HD), F32),
    ]
    out_specs = [here, here]
    scratch = []
    if first:
        out_shape += [
            jax.ShapeDtypeStruct((4,), jnp.int32),
            jax.ShapeDtypeStruct(full(heads * rows, HD), BF16),
            jax.ShapeDtypeStruct(full(rows, HD), BF16),
            jax.ShapeDtypeStruct(full(rows, HD), BF16),
        ]
        out_specs += [smem, here, here, here]
    else:
        aliases = {len(args) + i: (2 if last else 0) + i for i in range(2)}
        args += list(state)
        specs += [here, here]
    if last:
        group = heads * HD
        out_shape = [
            jax.ShapeDtypeStruct((rows, 2 * HALF_KV * group), BF16),
            jax.ShapeDtypeStruct((rows, group), BF16),
        ] + out_shape
        out_specs = [
            pl.BlockSpec((rows, group), lambda r, ids: (0, ids[0] * HALF_KV + head)),
            here,
        ] + out_specs
        if head:
            aliases[len(args)] = 0
            args.append(whole)
            specs.append(pl.BlockSpec(memory_space=pl.ANY))
        scratch = [
            pltpu.VMEM((rows, group), BF16),
            pltpu.VMEM((heads * rows, HD), F32),
            pltpu.VMEM((heads * rows, HD), F32),
        ]
    scratch += [
        pltpu.VMEM(((len(pieces_now) + 2) * count, HD), BF16),
        pltpu.VMEM(((len(pieces_now) + 2) * count, 2 * HD), BF16),
    ]
    return pl.pallas_call(
        functools.partial(
            stage_kernel,
            [chunk for _, _, chunk in pieces_now],
            [chunk for _, _, chunk in everything or ()],
            [part for _, part, _ in pieces],
            count,
            first,
            last,
            head,
        ),
        grid_spec=pltpu.PrefetchScalarGridSpec(
            num_scalar_prefetch=1,
            grid=(2,) if last else (HALF_KV, 2),
            in_specs=specs,
            out_specs=out_specs,
            scratch_shapes=scratch,
        ),
        out_shape=out_shape,
        input_output_aliases=aliases,
        compiler_params=pltpu.CompilerParams(vmem_limit_bytes=VMEM),
        cost_estimate=pl.CostEstimate(
            flops=15000000000 if first else 10000000000,
            bytes_accessed=1 << 18,
            transcendentals=0,
        ),
        name=name,
    )(*args)


def shards(
    prompt_queries,
    prompt_keys,
    prompt_values,
    cache_keys,
    cache_values,
    doc_blocks,
    reader_docs,
    reader_offsets,
):
    size = lax.axis_size("docs")
    me = lax.axis_index("docs").astype(jnp.int32)
    tokens = cache_keys.shape[0]
    half = lax.rem(me, 2)

    def moved(x, pairs):
        return lax.ppermute(
            x, "docs", [(i, j) for i, j in pairs if 0 <= i < size and 0 <= j < size]
        )

    everyone = range(size)
    second = lambda i: (i // 2) % 2
    beside = lambda x: moved(x, [(i, i ^ 1) for i in everyone])
    across = lambda x: moved(x, [(i, i ^ 2) for i in everyone])
    across_other = lambda x: moved(x, [(i, i ^ 3) for i in everyone])
    onward = lambda x: moved(x, [(i, i + 4) for i in everyone])
    onward_other = lambda x: moved(x, [(i, (i + 4) ^ 1) for i in everyone])
    back = lambda x: moved(x, [(i, i - 4) for i in everyone])
    back_other = lambda x: moved(x, [(i, (i - 4) ^ 1) for i in everyone])
    next_other = lambda x: moved(
        x, [(i, (i + 2) ^ 1 if second(i) else (i - 2) ^ 1) for i in everyone]
    )
    relay = lambda x: moved(x, [(i, i - 4 if second(i) else i + 4) for i in everyone])

    rows = prompt_queries.shape[0]
    block_rows = angle_rows(np.arange(COARSE) * BLK, attention_gain)
    coarse_rows = angle_rows(np.arange(COARSE) * COARSE, attention_gain)
    cache_table = np.concatenate(block_rows + angle_rows(np.arange(BLK), 1.0))
    query_table = np.concatenate(coarse_rows + angle_rows(np.arange(rows), 1.0))

    ids = jnp.stack([half, me * (tokens // BLK), me])
    columns = prompt_queries.shape[1] // 2
    width = prompt_keys.shape[1] // 2
    mine, theirs, message = prepare_cache(
        doc_blocks,
        reader_docs,
        reader_offsets,
        jnp.asarray(cache_table),
        cache_keys,
        cache_values,
        (prompt_queries, prompt_keys, prompt_values),
    )
    side = beside(message)
    other = beside(theirs)
    across_a = across(mine)
    chip = jnp.concatenate([mine, other], axis=0)
    onward_c = onward(chip)
    back_c = back(chip)
    across_b = across_other(lax.optimization_barrier((theirs, chip))[0])

    near = [(mine, 0, lambda i: i), (other, 0, lambda i: i ^ 1)]
    group = columns // HALF_KV
    mine_at = lambda k, r, ids: (0, ids[0] * HALF_KV + k)
    wide = lambda place: pl.BlockSpec((rows, group), place)
    thin = lambda place: pl.BlockSpec((rows, HD), place)
    table = jnp.asarray(query_table)
    inputs = [
        (doc_blocks, "scalar"),
        (reader_docs, "scalar"),
        (reader_offsets, "scalar"),
        (table, "whole"),
        (prompt_queries, wide(mine_at)),
        (prompt_keys, thin(mine_at)),
        (prompt_values, thin(mine_at)),
        (side, "whole"),
    ]
    kept = {"count": tokens, "rows": rows, "heads": group // HD}
    acc, bound, spans, turned_q, turned_k, kept_v = stage(
        ids, inputs, [], None, kept, name="alone"
    )
    bound, theirs, passing = lax.optimization_barrier((bound, theirs, across_a))
    far_a = relay(passing)
    far_b = next_other(theirs)
    kept.update(spans=spans, q=turned_q, k=turned_k, v=kept_v)
    middle = [
        (onward_c, 0, lambda i: i - 4),
        (onward_c, 1, lambda i: (i - 4) ^ 1),
        (across_a, 0, lambda i: i ^ 2),
        (across_b, 0, lambda i: i ^ 3),
        (back_c, 0, lambda i: i + 4),
        (back_c, 1, lambda i: (i + 4) ^ 1),
    ]
    state = stage(ids, [], near, (acc, bound), kept, name="near")
    state = stage(ids, [], middle, state, kept, name="middle")

    partner = lambda i: i - 2 + 4 * ((i >> 1) & 1)
    far = [(far_a, 0, partner), (far_b, 0, lambda i: partner(i) ^ 1)]
    everything = far + near + middle
    whole, sides = None, []
    for head in range(HALF_KV):
        whole, side_out, *state = stage(
            ids, [], far, state, kept, everything, head, whole, name="far"
        )
        sides.append(beside(side_out))
    for head, came in enumerate(sides):
        column = (1 - half) * columns + head * group
        whole = lax.dynamic_update_slice(whole, came, (jnp.int32(0), column))
    return whole


def solution(mesh):
    both = P(("groups", "docs"))
    wide = P(("groups", "docs"), None)
    placed = (wide, wide, wide, wide, wide, P("groups"), both, both)
    return jax.shard_map(shards, mesh=mesh, in_specs=placed, out_specs=wide, check_vma=False)
```

```python
import functools
import math

import jax
import jax.numpy as jnp
import numpy as np
from jax import lax
from jax.experimental import pallas as pl
from jax.experimental.pallas import tpu as pltpu
from jax.sharding import PartitionSpec as P

HD = 128
BLK = 32
HALF_KV = 2
F32 = jnp.float32
BF16 = jnp.bfloat16

rope_base = 1000000.0
yarn_factor = 4.0
pretrain_context = 32768.0
beta_fast = 32.0
beta_slow = 1.0
attention_gain = 0.1 * math.log(4.0) + 1.0
score_scale = 1.0 / math.sqrt(HD)
EXP2_SCALE = score_scale * math.log2(math.e)
SAFE_LOG2 = 60.0
masked_score = -1e30
ROW_TILE_HEADS = 4
VMEM = 28 * 1024 * 1024


def yarn_table():
    half = HD // 2

    def correction(turns):
        return (
            HD * math.log(pretrain_context / (turns * 2.0 * math.pi)) / (2.0 * math.log(rope_base))
        )

    lower = max(math.floor(correction(beta_fast)), 0)
    upper = min(math.ceil(correction(beta_slow)), HD - 1)
    span_width = max(upper - lower, 0.001)
    table = []
    for column in range(half):
        base_freq = rope_base ** (-2.0 * column / HD)
        fraction = min(max((column - lower) / span_width, 0.0), 1.0)
        table.append(base_freq * fraction / yarn_factor + base_freq * (1.0 - fraction))
    return np.asarray(table, np.float32).astype(np.float64)


def angle_rows(positions, gain):
    angles = np.asarray(positions, np.float64)[:, None] * yarn_table()[None, :]
    cosine = np.cos(angles) * gain
    sine = np.sin(angles) * gain
    return (
        np.concatenate([cosine, cosine], axis=1).astype(np.float32),
        np.concatenate([-sine, sine], axis=1).astype(np.float32),
    )


COARSE = 64


def cache_kernel(
    doc_blocks,
    doc,
    offset,
    table,
    k_ref,
    v_ref,
    q_all,
    k_all,
    v_all,
    mine_ref,
    theirs_ref,
    message,
):
    me = lax.axis_index("docs").astype(jnp.int32)
    half = lax.rem(me, 2)
    ndoc = doc_blocks.shape[0]
    width = HALF_KV * HD
    step = pl.program_id(0)
    @pl.when(step == 0)
    def _():
        place = 0
        for ref in (q_all, k_all, v_all):
            size = ref.shape[1] // 2
            col = pl.multiple_of((1 - half) * size, HD)
            message[:, place : place + size] = ref[:, pl.ds(col, size)]
            place += size
        at = jnp.clip(offset[0], 0, COARSE * COARSE - 1)
        hi = at // COARSE
        shape = (message.shape[0], HD)
        row = lax.broadcasted_iota(jnp.int32, shape, 0) // 16
        value = jnp.where(row == 0, doc[0], jnp.where(row == 1, hi, at - hi * COARSE))
        message[:, place : place + HD] = value.astype(F32).astype(BF16)

    blocks = k_ref.shape[0] // BLK
    first_block = me * blocks * pl.num_programs(0)
    c2 = table[2 * COARSE : 2 * COARSE + BLK, :]
    s2 = table[2 * COARSE + BLK : 2 * COARSE + 2 * BLK, :]
    for b in range(blocks):
        block = first_block + step * blocks + b

        def find(d, carry):
            start, begin = carry
            end = start + doc_blocks[d]
            return (end, jnp.where(start <= block, start, begin))

        _, begin = lax.fori_loop(0, ndoc, find, (jnp.int32(0), jnp.int32(0)), unroll=True)
        place = jnp.clip(block - begin, 0, COARSE - 1)
        c1 = table[pl.ds(place, 1), :]
        s1 = table[pl.ds(place + COARSE, 1), :]
        cosine = c1 * c2 - s1 * s2
        sine = s1 * c2 + c1 * s2
        rows = pl.ds(b * BLK, BLK)
        for out, which in ((mine_ref, half), (theirs_ref, 1 - half)):
            for j in range(HALF_KV):
                col = pl.multiple_of(which * width + j * HD, HD)
                x = k_ref[rows, pl.ds(col, HD)].astype(F32)
                y = x * cosine + pltpu.roll(x, HD // 2, 1) * sine
                out[rows, pl.ds(j * HD, HD)] = y.astype(BF16)
    for out, which in ((mine_ref, half), (theirs_ref, 1 - half)):
        col = pl.multiple_of(which * width, HD)
        out[:, pl.ds(width, width)] = v_ref[:, pl.ds(col, width)]


def prepare_cache(doc_blocks, doc, offset, table, keys, values, prompt):
    tokens, columns = keys.shape
    rows = prompt[0].shape[0]
    wide = sum(a.shape[1] // 2 for a in prompt) + HD
    steps = 2
    whole = lambda shape: pl.BlockSpec(shape, lambda i, *_: (0, 0))
    part = pl.BlockSpec((tokens // steps, columns), lambda i, *_: (i, 0))
    out = pl.BlockSpec((tokens // steps, columns), lambda i, *_: (i, 0))
    return pl.pallas_call(
        cache_kernel,
        grid_spec=pltpu.PrefetchScalarGridSpec(
            num_scalar_prefetch=3,
            grid=(steps,),
            in_specs=[whole(table.shape), part, part] + [whole(a.shape) for a in prompt],
            out_specs=[out, out, whole((rows, wide))],
        ),
        out_shape=[jax.ShapeDtypeStruct((tokens, columns), BF16)] * 2
        + [jax.ShapeDtypeStruct((rows, wide), BF16)],
        cost_estimate=pl.CostEstimate(flops=4000000, bytes_accessed=4 << 20, transcendentals=0),
        name="prepare_cache",
    )(doc_blocks, doc, offset, table, keys, values, *prompt)


def scores_of(q, k):
    return lax.dot_general(q, k, (((1,), (1,)), ((), ())), preferred_element_type=F32)


def square_bound(x):
    sums = jnp.dot(x * x, jnp.ones((HD, HD), BF16), preferred_element_type=F32)
    return jnp.max(sums.reshape(-1, 8, HD), axis=0)


def span_of(doc_blocks, doc):
    def find(d, carry):
        total, start, end = carry
        size = doc_blocks[d]
        start = jnp.where(d == doc, total, start)
        end = jnp.where(d == doc, total + size, end)
        return (total + size, start, end)

    zero = jnp.int32(0)
    _, start, end = lax.fori_loop(0, doc_blocks.shape[0], find, (zero, zero, zero), unroll=True)
    return start * BLK, end * BLK


def causal_mask(n):
    return lax.broadcasted_iota(jnp.int32, (n, n), 1) <= lax.broadcasted_iota(jnp.int32, (n, n), 0)


def whole_number(ref, place):
    return jnp.max(ref[16 * place : 16 * place + 16].astype(F32)).astype(jnp.int32)


def turning(table, offset_hi, offset_lo, rows):
    ca, sa = table[pl.ds(offset_hi, 1), :], table[pl.ds(offset_hi + COARSE, 1), :]
    cb = table[pl.ds(offset_lo + 2 * COARSE, 1), :]
    sb = table[pl.ds(offset_lo + 2 * COARSE + rows, 1), :]
    c1 = ca * cb - sa * sb
    s1 = sa * cb + ca * sb
    c2 = table[2 * COARSE : 2 * COARSE + rows, :]
    s2 = table[2 * COARSE + rows : 2 * COARSE + 2 * rows, :]
    return c1 * c2 - s1 * s2, s1 * c2 + c1 * s2


def stage_kernel(chunks, all_chunks, slots, count, first, last, head, *refs):
    refs = list(refs)
    take = lambda n: [refs.pop(0) for _ in range(n)]
    (ids,) = take(1)
    if first:
        doc_blocks, own_doc, own_offset, table, *own_reader, side = take(8)
    else:
        spans, q_ref, k_ref, v_ref = take(4)
    pieces = take(len(slots))
    if not first:
        acc_in, bound_in = take(2)
    if last:
        if head:
            take(1)
        own_out, side_out, acc_ref, bound_ref, out, peak_ref, total_ref = take(7)
    elif first:
        acc_ref, bound_ref, spans, q_ref, k_ref, v_ref = take(6)
    else:
        acc_ref, bound_ref = take(2)
    kbuf, vbuf = take(2)
    kvh = head if last else pl.program_id(0)
    reader = pl.program_id(0 if last else 1)
    me = ids[2]
    acc = acc_ref.at[reader, kvh]
    most = bound_ref.at[reader, kvh, 0:8]
    q_rows = q_ref.at[reader, kvh]
    k_own, v_own = k_ref.at[reader, kvh], v_ref.at[reader, kvh]
    rows = k_own.shape[0]

    def part(p, col):
        place = pl.ds(pl.multiple_of((col + kvh) * HD, HD), HD)
        return pieces[p][slots[p] * count : (slots[p] + 1) * count, place]

    heads = q_rows.shape[0] // rows
    tile = ROW_TILE_HEADS * rows
    tiles = heads // ROW_TILE_HEADS
    at = lambda t: slice(t * tile, (t + 1) * tile)

    if first:
        lead = 2 * heads

        def side_part(col):
            return side[:, pl.ds(pl.multiple_of(col * HD, HD), HD)]

        for r in range(2):

            @pl.when(reader == r)
            def _(r=r):
                if r == 0:
                    document = own_doc[0]
                    offset = jnp.clip(own_offset[0], 0, COARSE * COARSE - 1)
                    hi = offset // COARSE
                    lo = offset - hi * COARSE
                    raw_q = lambda h: own_reader[0][:, h * HD : (h + 1) * HD]
                    raw_k, raw_v = own_reader[1][...], own_reader[2][...]
                else:
                    numbers = side_part(lead + 2 * HALF_KV)
                    document, hi, lo = [whole_number(numbers, i) for i in range(3)]
                    raw_q = lambda h: side_part(kvh * heads + h)
                    raw_k, raw_v = side_part(lead + kvh), side_part(lead + HALF_KV + kvh)
                begin, finish = span_of(doc_blocks, document)
                spans[2 * r] = begin
                spans[2 * r + 1] = finish
                cosine, sine = turning(table, hi, lo, rows)

                def rotated(x):
                    x = x.astype(F32)
                    return (x * cosine + pltpu.roll(x, HD // 2, 1) * sine).astype(BF16)

                k_own[...] = rotated(raw_k)
                v_own[...] = raw_v
                for h in range(heads):
                    q_rows[h * rows : (h + 1) * rows, :] = rotated(raw_q(h))

    start = spans[2 * reader]
    end = spans[2 * reader + 1]

    if first:
        mask = jnp.concatenate([causal_mask(rows)] * ROW_TILE_HEADS, axis=0)
        keys = k_own[...]
        values = jnp.concatenate([v_own[...], jnp.ones((rows, HD), BF16)], axis=1)
        q_most = jnp.zeros((8, HD), F32)
        for t in range(tiles):
            q = q_rows[at(t), :]
            weights = jnp.exp2(scores_of(q, keys) * EXP2_SCALE)
            weights = jnp.where(mask, weights, 0.0).astype(BF16)
            acc[at(t), :] = jnp.dot(weights, values, preferred_element_type=F32)
            q_most = jnp.maximum(q_most, square_bound(q))
        most[...] = square_bound(keys)
        bound_ref[reader, kvh, 8:16, :] = q_most

    if not chunks:
        return
    filled = jnp.int32(0)
    for p in range(0, len(chunks), 2):
        bases = [chunks[p + i](me) * count for i in range(2)]
        lows = [jnp.maximum(base, start) for base in bases]
        shown = [
            jnp.maximum(jnp.minimum(base + count, end) - low, 0)
            for base, low in zip(bases, lows, strict=True)
        ]
        ahead = [jnp.where(bases[i] > bases[1 - i], shown[1 - i], 0) for i in range(2)]
        for i in range(2):

            @pl.when(shown[i] > 0)
            def _(p=p + i, put=count + filled + ahead[i] + bases[i] - lows[i]):
                to = pl.ds(pl.multiple_of(put, BLK), count)
                kbuf[to, :] = part(p, 0)
                vbuf[to, 0:HD] = part(p, HALF_KV)
                vbuf[to, HD:] = jnp.ones((count, HD), BF16)

        filled = filled + shown[0] + shown[1]
    some = filled > 0

    @pl.when(some)
    def _():
        to = pl.ds(pl.multiple_of(count + filled, BLK), count)
        kbuf[to, :] = jnp.zeros((count, HD), BF16)
        vbuf[to, :] = jnp.zeros((count, 2 * HD), BF16)

    def attend(step, _, size=count):
        here = pl.ds(pl.multiple_of(count + step * count, BLK), size)
        keys = kbuf[here, :]
        values = vbuf[here, :]
        most[...] = jnp.maximum(most[...], square_bound(keys))
        for t in range(tiles):
            weights = jnp.exp2(scores_of(q_rows[at(t), :], keys) * EXP2_SCALE).astype(BF16)
            acc[at(t), :] += jnp.dot(weights, values, preferred_element_type=F32)
        return 0

    half = count // 2
    steps = (filled + half - 1) // count
    lax.fori_loop(0, steps, attend, 0)

    @pl.when(filled > steps * count)
    def _():
        attend(steps, 0, half)

    if last:
        q_most = jnp.max(bound_ref[reader, kvh, 8:16, :])
        safe = jnp.max(most[...]) * q_most <= (SAFE_LOG2 / EXP2_SCALE) ** 2

        @pl.when(safe)
        def _():
            for h in range(heads):
                mine = slice(h * rows, (h + 1) * rows)
                out[:, h * HD : (h + 1) * HD] = (acc[mine, :HD] / acc[mine, HD:]).astype(BF16)

        @pl.when(jnp.logical_not(safe))
        def _():
            def absorb(h, keys, values, shown, fresh):
                mine = pl.ds(pl.multiple_of(h * rows, rows), rows)
                s = jnp.where(shown, scores_of(q_rows[mine, :], keys) * score_scale, masked_score)
                most_now = jnp.max(s, axis=1, keepdims=True)
                if fresh:
                    peak = jnp.broadcast_to(most_now, (rows, HD))
                else:
                    before = peak_ref[mine, :]
                    peak = jnp.maximum(before, most_now)
                w = jnp.where(shown, jnp.exp(s - peak[:, :1]), 0.0)
                total = jnp.broadcast_to(jnp.sum(w, axis=1, keepdims=True), (rows, HD))
                gained = jnp.dot(w.astype(BF16), values, preferred_element_type=F32)
                if not fresh:
                    factor = jnp.exp(before - peak)
                    total = total + total_ref[mine, :] * factor
                    gained = gained + acc[mine, 0:HD] * factor
                peak_ref[mine, :] = peak
                total_ref[mine, :] = total
                acc[mine, 0:HD] = gained

            def own(h, _):
                absorb(h, k_own[...], v_own[...], causal_mask(rows), True)
                return 0

            lax.fori_loop(0, heads, own, 0)
            for p, chunk in enumerate(all_chunks):
                base = chunk(me) * count

                @pl.when((base < end) & (base + count > start))
                def _(p=p, base=base):
                    token = base + lax.broadcasted_iota(jnp.int32, (rows, count), 1)
                    shown = (token >= start) & (token < end)

                    def body(h, _):
                        absorb(h, part(p, 0), part(p, HALF_KV), shown, False)
                        return 0

                    lax.fori_loop(0, heads, body, 0)

            def finish(h, _):
                mine = pl.ds(pl.multiple_of(h * rows, rows), rows)
                out[:, pl.ds(pl.multiple_of(h * HD, HD), HD)] = (
                    acc[mine, 0:HD] / total_ref[mine, :]
                ).astype(BF16)
                return 0

            lax.fori_loop(0, heads, finish, 0)

        for r, done in enumerate((own_out, side_out)):

            @pl.when(reader == r)
            def _(done=done):
                done[...] = out[...]


def stage(ids, inputs, pieces_now, state, kept, everything=None, head=0, whole=None, name="stage"):
    first = state is None
    last = everything is not None
    smem = pl.BlockSpec(memory_space=pltpu.SMEM)
    count = kept["count"]
    rows, heads = kept["rows"], kept["heads"]
    here = pl.BlockSpec(memory_space=pltpu.VMEM)
    pieces = everything or pieces_now
    args = [ids]
    specs = []
    for a, spec in inputs:
        args.append(a)
        specs.append(smem if spec == "scalar" else here if spec == "whole" else spec)
    if not first:
        args += [kept["spans"], kept["q"], kept["k"], kept["v"]]
        specs += [smem, here, here, here]
    args += [a for a, _, _ in pieces]
    specs += [here] * len(pieces)
    aliases = {}
    full = lambda *shape: (2, HALF_KV) + shape
    out_shape = [
        jax.ShapeDtypeStruct(full(heads * rows, 2 * HD), F32),
        jax.ShapeDtypeStruct(full(16, HD), F32),
    ]
    out_specs = [here, here]
    scratch = []
    if first:
        out_shape += [
            jax.ShapeDtypeStruct((4,), jnp.int32),
            jax.ShapeDtypeStruct(full(heads * rows, HD), BF16),
            jax.ShapeDtypeStruct(full(rows, HD), BF16),
            jax.ShapeDtypeStruct(full(rows, HD), BF16),
        ]
        out_specs += [smem, here, here, here]
    else:
        aliases = {len(args) + i: (2 if last else 0) + i for i in range(2)}
        args += list(state)
        specs += [here, here]
    if last:
        group = heads * HD
        out_shape = [
            jax.ShapeDtypeStruct((rows, 2 * HALF_KV * group), BF16),
            jax.ShapeDtypeStruct((rows, group), BF16),
        ] + out_shape
        out_specs = [
            pl.BlockSpec((rows, group), lambda r, ids: (0, ids[0] * HALF_KV + head)),
            here,
        ] + out_specs
        if head:
            aliases[len(args)] = 0
            args.append(whole)
            specs.append(pl.BlockSpec(memory_space=pl.ANY))
        scratch = [
            pltpu.VMEM((rows, group), BF16),
            pltpu.VMEM((heads * rows, HD), F32),
            pltpu.VMEM((heads * rows, HD), F32),
        ]
    scratch += [
        pltpu.VMEM(((len(pieces_now) + 2) * count, HD), BF16),
        pltpu.VMEM(((len(pieces_now) + 2) * count, 2 * HD), BF16),
    ]
    return pl.pallas_call(
        functools.partial(
            stage_kernel,
            [chunk for _, _, chunk in pieces_now],
            [chunk for _, _, chunk in everything or ()],
            [part for _, part, _ in pieces],
            count,
            first,
            last,
            head,
        ),
        grid_spec=pltpu.PrefetchScalarGridSpec(
            num_scalar_prefetch=1,
            grid=(2,) if last else (HALF_KV, 2),
            in_specs=specs,
            out_specs=out_specs,
            scratch_shapes=scratch,
        ),
        out_shape=out_shape,
        input_output_aliases=aliases,
        compiler_params=pltpu.CompilerParams(vmem_limit_bytes=VMEM),
        cost_estimate=pl.CostEstimate(
            flops=15000000000 if first else 10000000000,
            bytes_accessed=1 << 18,
            transcendentals=0,
        ),
        name=name,
    )(*args)


def shards(
    prompt_queries,
    prompt_keys,
    prompt_values,
    cache_keys,
    cache_values,
    doc_blocks,
    reader_docs,
    reader_offsets,
):
    size = lax.axis_size("docs")
    me = lax.axis_index("docs").astype(jnp.int32)
    tokens = cache_keys.shape[0]
    half = lax.rem(me, 2)

    def moved(x, pairs):
        return lax.ppermute(
            x, "docs", [(i, j) for i, j in pairs if 0 <= i < size and 0 <= j < size]
        )

    everyone = range(size)
    second = lambda i: (i // 2) % 2
    beside = lambda x: moved(x, [(i, i ^ 1) for i in everyone])
    across = lambda x: moved(x, [(i, i ^ 2) for i in everyone])
    across_other = lambda x: moved(x, [(i, i ^ 3) for i in everyone])
    onward = lambda x: moved(x, [(i, i + 4) for i in everyone])
    onward_other = lambda x: moved(x, [(i, (i + 4) ^ 1) for i in everyone])
    back = lambda x: moved(x, [(i, i - 4) for i in everyone])
    back_other = lambda x: moved(x, [(i, (i - 4) ^ 1) for i in everyone])
    next_other = lambda x: moved(
        x, [(i, (i + 2) ^ 1 if second(i) else (i - 2) ^ 1) for i in everyone]
    )
    relay = lambda x: moved(x, [(i, i - 4 if second(i) else i + 4) for i in everyone])

    rows = prompt_queries.shape[0]
    block_rows = angle_rows(np.arange(COARSE) * BLK, attention_gain)
    coarse_rows = angle_rows(np.arange(COARSE) * COARSE, attention_gain)
    cache_table = np.concatenate(block_rows + angle_rows(np.arange(BLK), 1.0))
    query_table = np.concatenate(coarse_rows + angle_rows(np.arange(rows), 1.0))

    ids = jnp.stack([half, me * (tokens // BLK), me])
    columns = prompt_queries.shape[1] // 2
    width = prompt_keys.shape[1] // 2
    mine, theirs, message = prepare_cache(
        doc_blocks,
        reader_docs,
        reader_offsets,
        jnp.asarray(cache_table),
        cache_keys,
        cache_values,
        (prompt_queries, prompt_keys, prompt_values),
    )
    side = beside(message)
    other = beside(theirs)
    across_a = across(mine)
    chip = jnp.concatenate([mine, other], axis=0)
    onward_c = onward(chip)
    back_c = back(chip)
    across_b = across_other(lax.optimization_barrier((theirs, chip))[0])

    near = [(mine, 0, lambda i: i), (other, 0, lambda i: i ^ 1)]
    group = columns // HALF_KV
    mine_at = lambda k, r, ids: (0, ids[0] * HALF_KV + k)
    wide = lambda place: pl.BlockSpec((rows, group), place)
    thin = lambda place: pl.BlockSpec((rows, HD), place)
    table = jnp.asarray(query_table)
    inputs = [
        (doc_blocks, "scalar"),
        (reader_docs, "scalar"),
        (reader_offsets, "scalar"),
        (table, "whole"),
        (prompt_queries, wide(mine_at)),
        (prompt_keys, thin(mine_at)),
        (prompt_values, thin(mine_at)),
        (side, "whole"),
    ]
    kept = {"count": tokens, "rows": rows, "heads": group // HD}
    acc, bound, spans, turned_q, turned_k, kept_v = stage(
        ids, inputs, [], None, kept, name="alone"
    )
    bound, theirs, passing = lax.optimization_barrier((bound, theirs, across_a))
    far_a = relay(passing)
    far_b = next_other(theirs)
    kept.update(spans=spans, q=turned_q, k=turned_k, v=kept_v)
    middle = [
        (onward_c, 0, lambda i: i - 4),
        (onward_c, 1, lambda i: (i - 4) ^ 1),
        (across_a, 0, lambda i: i ^ 2),
        (across_b, 0, lambda i: i ^ 3),
        (back_c, 0, lambda i: i + 4),
        (back_c, 1, lambda i: (i + 4) ^ 1),
    ]
    state = stage(ids, [], near, (acc, bound), kept, name="near")
    state = stage(ids, [], middle, state, kept, name="middle")

    partner = lambda i: i - 2 + 4 * ((i >> 1) & 1)
    far = [(far_a, 0, partner), (far_b, 0, lambda i: partner(i) ^ 1)]
    everything = far + near + middle
    whole, sides = None, []
    for head in range(HALF_KV):
        whole, side_out, *state = stage(
            ids, [], far, state, kept, everything, head, whole, name="far"
        )
        sides.append(beside(side_out))
    for head, came in enumerate(sides):
        column = (1 - half) * columns + head * group
        whole = lax.dynamic_update_slice(whole, came, (jnp.int32(0), column))
    return whole


def solution(mesh):
    both = P(("groups", "docs"))
    wide = P(("groups", "docs"), None)
    placed = (wide, wide, wide, wide, wide, P("groups"), both, both)
    return jax.shard_map(shards, mesh=mesh, in_specs=placed, out_specs=wide, check_vma=False)
```
